256 devices in a mesh: rep: 16 (over z, y_hi), section: 4 (over y_lo, core), head: 4 (over x).
Axes of the slice: x: 4, y: 4 (y_hi: 2, y_lo: 2; y = y_hi * 2 + y_lo), z: 8, core: 2. Of those that a mesh axis runs over, the one named last changes fastest.
Arguments:
- prompt_pages: bfloat16 [16, 4, 16, 16, 2, 6144], P('rep', 'section', 'head'), may hold values from -6 to 6
- page_scales: bfloat16 [16, 4, 16, 2, 48], P('rep', 'section', 'head'), may hold values from 0.099609375 to 1.5
- page_table: int32 [16, 16], P('rep'), may hold values from 0 to 15, each once within a row
- lengths: int32 [16, 8], replicated, may hold values from 1 to 32, 160 in all within a row
- route: int32 [16, 8], replicated, may hold values from 0 to 15, as said below
- queries: bfloat16 [16, 4, 16, 2, 8, 6144], P('rep', None, None, None, None, ('section', 'head')), may hold values from -6 to 6
- new_kv: bfloat16 [16, 4, 16, 2, 8, 2, 6144], P('rep', None, None, None, None, None, ('section', 'head')), may hold values from -6 to 6
Outputs:
- decode_cache: bfloat16 [16, 4, 16, 2, 32, 2, 6144], P('rep', None, None, None, None, None, ('section', 'head'))
- decode_scales: bfloat16 [16, 4, 16, 2, 2, 2, 48], P('rep', None, None, None, None, None, ('section', 'head'))
- attention: bfloat16 [16, 4, 16, 2, 8, 6144], P('rep', None, None, None, None, ('section', 'head'))
The draws below stay inside these ranges and needn't reach their ends.
Inputs may be any that keep to these rules, and one draw needn't show every extreme that they name: `page_table`: each row is a permutation of one instance's 16 page slots; page j of request q is entry q * 2 + j. `lengths`: each row sums to 160 and holds one length 32. `route`: no replica gets more than 2 requests of one instance, and in every draw one replica gets exactly 2 from every instance.
All inputs are finite; a program needn't handle non-finite values.
Results may differ from the reference program's by a relative error of at most 0.0049.
Values may be sent and summed in bfloat16 or wider, within the bound.
A program may use at most 128 MiB of HBM per device.

```python
import math
import jax
import jax.numpy as jnp
import numpy as np
from jax import lax

HEADS = 48
HEAD_DIM = 128
PAGE = 16
PAGES_REQ = 2
REQ = 8
STEPS = 8
LAYERS = 4
CAP = 2
LMAX = 32
NPAGE = 16
WIDTH = 6144
N_REP = 16


def draw_new_kv(key, part):
    key = jax.random.fold_in(key, 7)
    full_shape = (N_REP, LAYERS, N_REP, CAP, STEPS, 2, WIDTH)
    return jnp.clip(jax.random.normal(key, full_shape, jnp.float32), -6.0, 6.0).astype(jnp.bfloat16)


def draw_queries(key, part):
    key = jax.random.fold_in(key, 9)
    full_shape = (N_REP, LAYERS, N_REP, CAP, STEPS, WIDTH)
    return jnp.clip(jax.random.normal(key, full_shape, jnp.float32), -6.0, 6.0).astype(jnp.bfloat16)


def draw_route(key, part):
    key = jax.random.fold_in(key, 5)
    key_hot, key_rest = jax.random.split(key)
    hot_replica = jax.random.randint(key_hot, (), 0, N_REP)
    slot_count = N_REP * CAP
    slot_owner = jnp.arange(slot_count, dtype=jnp.int32) // CAP

    def instance_routes(sub_key):
        key_order, key_shuffle = jax.random.split(sub_key)
        shuffled = jax.random.permutation(key_order, slot_count)
        position = jnp.argsort(shuffled)
        priority = jnp.where(slot_owner == hot_replica, 0, 1 + position)
        chosen = slot_owner[jnp.argsort(priority, stable=True)][:REQ]
        return jax.random.permutation(key_shuffle, chosen)
    return jax.vmap(instance_routes)(jax.random.split(key_rest, N_REP)).astype(jnp.int32)


def level_of(key, dims, cuts, least, largest):
    def one(axis_at, parts):
        heights = jax.random.uniform(jax.random.fold_in(jax.random.fold_in(key, 6), axis_at), (parts,), jnp.float32, least / len(cuts), largest / len(cuts))
        return jnp.repeat(jnp.exp(heights), dims[axis_at] // parts).reshape((-1,) + (1,) * (len(dims) - axis_at - 1))

    factor_of = one(*cuts[0])
    for cut in cuts[1:]:
        factor_of = factor_of * one(*cut)
    return factor_of


def length_profile(amount, total, most, skew):
    portions = [(1 << 20) // math.isqrt(grade ** skew) + 1 for grade in range(2, amount + 1)]
    spare, given = total - most - (amount - 1), [1] * (amount - 1)
    while spare > 0:
        free = [i for i in range(amount - 1) if given[i] < most]
        whole, left = sum([portions[i] for i in free]), spare
        for i in free:
            extra = min(most - given[i], max(1, left * portions[i] // whole), spare)
            given[i] = given[i] + extra
            spare = spare - extra
    return np.array([most] + given)


def uneven_parts(rng, amount, total, reach, skew):
    if amount == 2:
        one = jax.random.randint(rng, (), max(1, total - reach), min(reach, total - 1) + 1)
        return jnp.stack([one, total - one])
    tallies = jnp.asarray(length_profile(amount, total, reach, skew), jnp.int32)
    twos = (amount - 1) // 2
    donor, receiver = tallies[1:1 + 2 * twos:2], tallies[2:2 + 2 * twos:2]
    slack = jnp.minimum(donor - 1, reach - receiver)
    shifted = jax.random.randint(jax.random.fold_in(rng, 1), (twos,), 0, 1 << 20) % (slack + 1)
    tallies = tallies.at[1:1 + 2 * twos:2].set(donor - shifted).at[2:2 + 2 * twos:2].set(receiver + shifted)
    return tallies[jax.random.permutation(jax.random.fold_in(rng, 2), amount)]


def centred(rng, shape, spread, reach, shards=(), held_as=jnp.bfloat16):
    values = spread * jax.random.normal(rng, shape, jnp.float32)
    if shards:
        values = values * level_of(rng, shape, shards, -0.22, 0.18)
    return jnp.clip(values, -reach, reach).astype(held_as)


def setup_inputs(seed: int = 0) -> dict:
    arg_keys = jax.random.split(jax.random.key(seed), 8)
    return {
        "prompt_pages": centred(arg_keys[0], (N_REP, LAYERS, NPAGE, PAGE, 2, WIDTH), 1.0, 6.0, ((0, 16), (1, 4), (2, 4))),
        "page_scales": jnp.clip(jnp.exp(math.log(1.5) - 2.7119641 * jax.random.uniform(arg_keys[1], (N_REP, LAYERS, NPAGE, 2, HEADS), jnp.float32) ** level_of(arg_keys[1], (N_REP, LAYERS, NPAGE, 2, HEADS), ((0, 16), (1, 4), (2, 4)), -0.2, 0.2)), 0.099609375, 1.5).astype(jnp.bfloat16),
        "page_table": jax.vmap(lambda own: jax.random.permutation(own, NPAGE))(jax.random.split(arg_keys[2], N_REP)).reshape((N_REP, NPAGE)).astype(jnp.int32),
        "lengths": jax.vmap(lambda own: uneven_parts(own, REQ, REQ * LMAX * 5 // 8, LMAX, 2))(jax.random.split(arg_keys[3], N_REP)).reshape((N_REP, REQ)).astype(jnp.int32),
        "route": draw_route(jax.random.fold_in(arg_keys[7], 71), 0),
        "queries": draw_queries(jax.random.fold_in(arg_keys[7], 71), 0),
        "new_kv": draw_new_kv(jax.random.fold_in(arg_keys[7], 71), 0),
    }


def reference(prompt_pages, page_scales, page_table, lengths, route, queries, new_kv):
    req_ids = jnp.arange(REQ, dtype=jnp.int32)
    same_dest = route[:, :, None] == route[:, None, :]
    earlier = req_ids[None, :] < req_ids[:, None]
    slot_rank = lax.optimization_barrier(jnp.sum((same_dest & earlier[None]).astype(jnp.int32), axis=2))
    dest_ids = jnp.arange(N_REP, dtype=jnp.int32)
    cap_ids = jnp.arange(CAP, dtype=jnp.int32)
    slot_match = (route[None, :, None, :] == dest_ids[:, None, None, None]) & (slot_rank[None, :, None, :] == cap_ids[None, None, :, None])
    slot_live = jnp.any(slot_match, axis=3)
    slot_request = lax.optimization_barrier(jnp.sum(jnp.where(slot_match, req_ids[None, None, None, :], 0), axis=3)).astype(jnp.int32)
    slot_length = lax.optimization_barrier(jnp.sum(jnp.where(slot_match, lengths[None, :, None, :], 0), axis=3)).astype(jnp.int32)
    page_ids = jnp.arange(PAGES_REQ, dtype=jnp.int32)
    instance = jnp.arange(N_REP, dtype=jnp.int32)
    physical = page_table[instance[None, :, None, None], slot_request[..., None] * PAGES_REQ + page_ids].astype(jnp.int32)
    score_root = math.sqrt(HEAD_DIM)

    def per_replica(destination):
        phys_here = physical[destination]
        live_here = slot_live[destination]
        span_here = slot_length[destination]
        slot_pages = prompt_pages[instance[:, None, None], :, phys_here]
        slot_pages = jnp.where(live_here[:, :, None, None, None, None, None], slot_pages, jnp.zeros((), slot_pages.dtype))
        page_cache = jnp.transpose(slot_pages, (3, 0, 1, 2, 4, 5, 6)).reshape(LAYERS, N_REP, CAP, LMAX, 2, WIDTH)
        slot_scales = page_scales[instance[:, None, None], :, phys_here]
        slot_scales = jnp.where(live_here[:, :, None, None, None, None], slot_scales, jnp.zeros((), slot_scales.dtype))
        scale_cache = jnp.transpose(slot_scales, (3, 0, 1, 2, 4, 5))
        query_rows = queries[destination].astype(jnp.float32).reshape(LAYERS, N_REP, CAP, STEPS, HEADS, HEAD_DIM)
        new_tokens = new_kv[destination].astype(jnp.float32).reshape(LAYERS, N_REP, CAP, STEPS, 2, HEADS, HEAD_DIM)
        prompt_keys = page_cache[:, :, :, :, 0, :].astype(jnp.float32).reshape(LAYERS, N_REP, CAP, LMAX, HEADS, HEAD_DIM)
        prompt_values = page_cache[:, :, :, :, 1, :].astype(jnp.float32).reshape(LAYERS, N_REP, CAP, LMAX, HEADS, HEAD_DIM)
        key_scale = jnp.transpose(jnp.repeat(scale_cache[:, :, :, :, 0, :], PAGE, axis=3), (0, 1, 2, 4, 3))[:, :, :, :, None, :]
        value_scale = jnp.transpose(jnp.repeat(scale_cache[:, :, :, :, 1, :], PAGE, axis=3), (0, 1, 2, 4, 3))[:, :, :, :, None, :]
        prompt_score = jnp.einsum('lrcthd,lrckhd->lrchtk', query_rows, prompt_keys) * key_scale.astype(jnp.float32) / score_root
        fresh_score = jnp.einsum('lrcthd,lrcuhd->lrchtu', query_rows, new_tokens[:, :, :, :, 0]) / score_root
        visible = (jnp.arange(LMAX, dtype=jnp.int32)[None, None, :] < span_here[:, :, None])[None, :, :, None, None, :]
        causal = jnp.arange(STEPS, dtype=jnp.int32)[None, :] <= jnp.arange(STEPS, dtype=jnp.int32)[:, None]
        row_max = jnp.maximum(lax.optimization_barrier(jnp.max(jnp.where(visible, prompt_score, -jnp.inf), axis=-1, keepdims=True)), lax.optimization_barrier(jnp.max(jnp.where(causal, fresh_score, -jnp.inf), axis=-1, keepdims=True)))
        exp_prompt = jnp.where(visible, jnp.exp(prompt_score - row_max), 0.0)
        exp_fresh = jnp.where(causal, jnp.exp(fresh_score - row_max), 0.0)
        row_total = lax.optimization_barrier(jnp.sum(exp_prompt, axis=-1, keepdims=True)) + lax.optimization_barrier(jnp.sum(exp_fresh, axis=-1, keepdims=True))
        prompt_weight = (exp_prompt * value_scale.astype(jnp.float32) / row_total).astype(jnp.bfloat16)
        fresh_weight = (exp_fresh / row_total).astype(jnp.bfloat16)
        attended = jnp.einsum('lrchtk,lrckhd->lrcthd', prompt_weight.astype(jnp.float32), prompt_values)
        attended = attended + jnp.einsum('lrchtu,lrcuhd->lrcthd', fresh_weight.astype(jnp.float32), new_tokens[:, :, :, :, 1])
        attended = jnp.where(live_here[None, :, :, None, None, None], attended, 0.0)
        attended = attended.astype(jnp.bfloat16).reshape(LAYERS, N_REP, CAP, STEPS, WIDTH)
        return (page_cache, scale_cache, attended)
    decode_cache, decode_scales, attention = lax.map(per_replica, dest_ids)
    return (decode_cache, decode_scales, attention)
```

```python
import math

import jax
import jax.numpy as jnp
import numpy as np
from jax import lax
from jax.experimental import pallas as pl
from jax.experimental.pallas import tpu as pltpu
from jax.sharding import PartitionSpec as P

MESH = pl.DeviceIdType.MESH
NODES = 16
RING = NODES // 2
PORTS = 3
ROUNDS = 16
PARTS = 4
REQS = 8
STORE = REQS + PORTS * ROUNDS

ROUTES = (
    0o5555555222222210, 0o5555555222222201, 0o4645121222121045, 0o5555212221210154,
    0o4612132222104545, 0o5531222222015554, 0o2212122210555646, 0o3121222101545455,
    0o1313121055555512, 0o2222210155555451, 0o1312105545565515, 0o2222015455555521,
    0o1310554545561212, 0o2201555555542221, 0o1055555555121212, 0o0155555454222222,
    0o5555552522222210, 0o5555552522222201, 0o5546222322221045, 0o5555522122220154,
    0o4526221222105645, 0o2122312131015554, 0o4323221310464555, 0o2232312101646565,
    0o2222231045454555, 0o3122220155646521, 0o2222105556454623, 0o3131015555542231,
    0o2210455656452312, 0o2101555564555232, 0o1045455546131312, 0o0154546565312122,
)


def links_of(source, dest, code):
    if code == 0:
        return []
    z, y = divmod(source, 2)
    step, mode = (1, (code - 1) % 3) if code <= 3 else (-1, (code - 1) % 3)
    cross = y != dest % 2
    hops = [2] if (cross and mode == 0) or (not cross and mode == 2) else []
    hops += [0 if step > 0 else 1] * (((dest // 2 - z) * step) % RING)
    if (cross and mode != 0) or (not cross and mode == 2):
        hops += [2]
    links = []
    for port in hops:
        links.append((z * 2 + y) * PORTS + port)
        if port == 2:
            y = 1 - y
        else:
            z = (z + (1 if port == 0 else -1)) % RING
    assert z * 2 + y == dest and len(links) < 8
    return links


def path_table():
    table = np.zeros((2, NODES, 8, NODES), np.float32)
    for rank in range(2):
        for source in range(NODES):
            for dest in range(NODES):
                code = (ROUTES[rank * NODES + source] >> (3 * dest)) & 7
                for hop, link in enumerate(links_of(source, dest, code)):
                    table[rank, dest, hop, source] = link + 1
    return table.reshape(2 * NODES * 8, NODES)


def plan_kernel(table_ref, route_ref, length_ref, out_ref, sends):
    f32 = jnp.float32
    lane = lax.broadcasted_iota(jnp.int32, (1, 128), 1)
    route = route_ref[...]
    source = lane // REQS
    order = lane % REQS
    rank = jnp.zeros_like(route)
    for back in range(1, REQS):
        earlier = pltpu.roll(route, back, axis=1)
        rank = rank + jnp.where((earlier == route) & (order >= back), 1, 0)
    node = lax.broadcasted_iota(jnp.int32, (NODES, 128), 0)
    count = jnp.sum(jnp.where(node == route, 1.0, 0.0), axis=1, keepdims=True)
    most = jnp.max(count, axis=0, keepdims=True)
    nodes = lax.broadcasted_iota(jnp.int32, (NODES, 1), 0).astype(f32)
    hot = jnp.min(jnp.where(count == most, nodes, 99.0), axis=0, keepdims=True).astype(jnp.int32)
    hot_z, hot_y = hot // 2, hot % 2

    def relative(x):
        y = x % 2
        return ((x // 2 - hot_z + RING) % RING) * 2 + (y + hot_y - 2 * y * hot_y)

    source_rel, dest_rel = relative(source), relative(route)
    from_one = jnp.where(node == source_rel, 1.0, 0.0).astype(jnp.bfloat16)
    every = jnp.dot(table_ref[...], from_one, preferred_element_type=f32)
    row = lax.broadcasted_iota(jnp.int32, (2 * NODES * 8, 128), 0) // 8
    every = jnp.where(row == rank * NODES + dest_rel, every, 0.0)
    path = every[0:8]
    for i in range(1, 2 * NODES):
        path = path + every[8 * i : 8 * i + 8]
    me = relative(jnp.zeros((1, 1), jnp.int32) + lax.axis_index("rep"))
    me_z, me_y = me // 2, me % 2
    up, down = (me_z + 1) % RING, (me_z + RING - 1) % RING
    to_me = (down * 2 + me_y, up * 2 + me_y, me_z * 2 + 1 - me_y)
    out_link = [(me * PORTS + k + 1).astype(f32) for k in range(PORTS)]
    in_link = [(to_me[k] * PORTS + k + 1).astype(f32) for k in range(PORTS)]
    link = lax.broadcasted_iota(jnp.int32, (NODES * PORTS, 128), 0).astype(f32) + 1.0
    tie = (127 - lane).astype(f32)
    hop_row = lax.broadcasted_iota(jnp.int32, (8, 128), 0)
    held = jnp.where(source_rel == me, order, 0).astype(f32)
    sends[...] = jnp.zeros_like(sends)
    for t in range(ROUNDS):
        now = path[0:1]
        left = jnp.sum(jnp.where(path > 0.0, 1.0, 0.0), axis=0, keepdims=True)
        key = left * 128.0 + tie
        asks = link == now
        first = jnp.max(jnp.where(asks, key, -1.0), axis=1, keepdims=True)
        wins = jnp.where(asks & (first == key), 1.0, 0.0)
        moves = jnp.max(wins, axis=0, keepdims=True) > 0.0
        for k in range(PORTS):
            leaves = moves & (now == out_link[k])
            sends[PORTS * t + k : PORTS * t + k + 1] = jnp.where(leaves, held, 0.0)
        for k in range(PORTS):
            held = jnp.where(moves & (now == in_link[k]), float(REQS + PORTS * t + k), held)
        later = jnp.where(hop_row < 7, pltpu.roll(path, 7, axis=0), 0.0)
        path = jnp.where(moves, later, path)
    left = jnp.sum(jnp.where(path > 0.0, 1.0, 0.0), axis=0, keepdims=True)
    stuck = jnp.sum(left, axis=1, keepdims=True)
    square = lax.broadcasted_iota(jnp.int32, (128, 128), 0) == lax.broadcasted_iota(
        jnp.int32, (128, 128), 1
    )

    def lay(rows):
        sums = jnp.sum(rows, axis=1, keepdims=True)
        n = rows.shape[0]
        return jnp.sum(jnp.where(square[:n], sums, 0.0), axis=0, keepdims=True)

    slot = lax.broadcasted_iota(jnp.int32, (2 * NODES, 128), 0)
    mine = (slot == source * 2 + rank) & (dest_rel == me)
    out = [
        lay(sends[...]),
        lay(jnp.where(mine, held, 0.0)),
        lay(jnp.where(mine, length_ref[...].astype(f32), 0.0)),
        jnp.where(lane >= 0, jnp.where(stuck > 0.0, 0.0, 1.0), 0.0),
        jnp.zeros((4, 128), f32),
    ]
    out_ref[...] = jnp.concatenate(out, axis=0).astype(jnp.int32)


def plan(route, lengths):
    return pl.pallas_call(
        plan_kernel,
        out_shape=jax.ShapeDtypeStruct((8, 128), jnp.int32),
        in_specs=[pl.BlockSpec(memory_space=pltpu.VMEM)] * 3,
        out_specs=pl.BlockSpec(memory_space=pltpu.VMEM),
        scratch_shapes=[pltpu.VMEM((128, 128), jnp.float32)],
    )(
        jnp.asarray(path_table(), jnp.bfloat16),
        route.reshape(1, 128),
        lengths.reshape(1, 128),
    )


def exchange_kernel(plan_ref, table_ref, pages, scales, *refs):
    streams = PARTS + 1
    outs = refs[:streams]
    groups = refs[streams : 2 * streams]
    stores = refs[2 * streams : 3 * streams]
    lands = refs[3 * streams : 4 * streams]
    packs = refs[4 * streams : 5 * streams]
    group_send, group_recv, send_sem, recv_sem, out_sem = refs[5 * streams :]
    rep = lax.axis_index("rep")
    section = lax.axis_index("section")
    head = lax.axis_index("head")
    tokens = groups[0].shape[2]
    held = pages.shape[2]
    feats = groups[0].shape[4]

    peers = []
    for o in range(16):
        peers.append((lax.rem(section + o // 4, 4), lax.rem(head + o % 4, 4)))
    neighbours = (
        lax.rem(rep + 2, NODES),
        lax.rem(rep + NODES - 2, NODES),
        rep + 1 - 2 * lax.rem(rep, 2),
    )
    barrier = pltpu.get_barrier_semaphore()
    for s, h in peers[1:]:
        pl.semaphore_signal(barrier, inc=1, device_id=(rep, s, h), device_id_type=MESH)
    for n in neighbours:
        pl.semaphore_signal(barrier, inc=1, device_id=(n, section, head), device_id_type=MESH)
    pl.semaphore_wait(barrier, 15 + PORTS)

    def block(i, group):
        if i == PARTS:
            return scales.at[group]
        columns = pl.ds(pl.multiple_of(group * feats, 128), feats)
        return pages.at[0, 0, :, pl.ds(tokens * i, tokens), :, columns]

    def place(i, s, h):
        return groups[i].at[s, pl.ds(held * h, held)]

    def regroup(i, o):
        s, h = peers[o]
        return pltpu.make_async_remote_copy(
            src_ref=block(i, s * 4 + h),
            dst_ref=place(i, section, head),
            send_sem=group_send.at[i, o],
            recv_sem=group_recv.at[i, o],
            device_id=(rep, s, h),
            device_id_type=MESH,
        )

    def regroup_own(i):
        return pltpu.make_async_copy(
            block(i, section * 4 + head), place(i, section, head), group_recv.at[i, 0]
        )

    order = [PARTS] + list(range(PARTS))
    for i in order:
        for o in range(1, 16):
            regroup(i, o).start()
        regroup_own(i).start()

    def send(i, slot, k):
        return pltpu.make_async_remote_copy(
            src_ref=packs[i].at[slot, k],
            dst_ref=lands[i].at[slot, k],
            send_sem=send_sem.at[i, slot, k],
            recv_sem=recv_sem.at[i, slot, k],
            device_id=(neighbours[k], section, head),
            device_id_type=MESH,
        )

    def write_own(i):
        return pltpu.make_async_copy(
            stores[i].at[pl.ds(0, REQS)], outs[i].at[pl.ds(0, REQS)], out_sem.at[i]
        )

    def write(i, t):
        rows = pl.ds(REQS + PORTS * t, PORTS)
        return pltpu.make_async_copy(stores[i].at[rows], outs[i].at[rows], out_sem.at[i])

    def compose(i, t, slot):
        for k in range(PORTS):
            packs[i][slot, k] = stores[i][plan_ref[0, PORTS * t + k]]
        for k in range(PORTS):
            send(i, slot, k).start()

    def arrive(i, t, slot):
        for k in range(PORTS):
            send(i, slot, k).wait_recv()
        for k in range(PORTS):
            stores[i][REQS + PORTS * t + k] = lands[i][slot, k]

    for i in order:
        regroup_own(i).wait()
        for o in range(1, 16):
            regroup(i, o).wait_recv()
        for q in range(REQS):
            for j in range(2):
                stores[i][q, :, j] = groups[i][:, table_ref[0, 2 * q + j]]
        write_own(i).start()
        compose(i, 0, 0)

    for i in order:
        arrive(i, 0, 0)
        write_own(i).wait()
        write(i, 0).start()
        compose(i, 1, 1)

    def one(t, carry):
        slot = lax.rem(t, 2)
        for i in order:
            arrive(i, t - 1, 1 - slot)
            write(i, t - 2).wait()
            write(i, t - 1).start()
            for k in range(PORTS):
                send(i, slot, k).wait_send()
            compose(i, t, slot)
        return carry

    lax.fori_loop(2, ROUNDS, one, 0)
    for i in order:
        arrive(i, ROUNDS - 1, (ROUNDS - 1) % 2)
        write(i, ROUNDS - 2).wait()
        write(i, ROUNDS - 1).start()
    for i in order:
        write(i, ROUNDS - 1).wait()
        for slot in range(2):
            for k in range(PORTS):
                send(i, slot, k).wait_send()
        for o in range(1, 16):
            regroup(i, o).wait_send()


def exchange(steps, page_table, pages, scales):
    layers = 4
    held = pages.shape[2]
    tokens = pages.shape[3] // PARTS
    feats = pages.shape[5] // 16
    units = [(tokens, 2, feats)] * PARTS + [(2, 128)]
    bf16 = jnp.bfloat16
    anywhere = pl.BlockSpec(memory_space=pl.ANY)
    smem = pl.BlockSpec(memory_space=pltpu.SMEM)
    scratch = [pltpu.VMEM((layers, 4 * held) + u, bf16) for u in units]
    scratch += [pltpu.VMEM((STORE, layers, 2) + u, bf16) for u in units]
    scratch += [pltpu.VMEM((2, PORTS, layers, 2) + u, bf16) for u in units] * 2
    dma = pltpu.SemaphoreType.DMA
    streams = PARTS + 1
    scratch += [dma((streams, 16)), dma((streams, 16))]
    scratch += [dma((streams, 2, PORTS)), dma((streams, 2, PORTS)), dma((streams,))]
    return pl.pallas_call(
        exchange_kernel,
        out_shape=[jax.ShapeDtypeStruct((STORE, layers, 2) + u, bf16) for u in units],
        in_specs=[smem, smem, anywhere, anywhere],
        out_specs=[anywhere] * streams,
        scratch_shapes=scratch,
        compiler_params=pltpu.CompilerParams(
            collective_id=1, has_side_effects=True, vmem_limit_bytes=40 << 20
        ),
        cost_estimate=pl.CostEstimate(flops=0, bytes_accessed=20 << 20, transcendentals=0),
    )(steps, page_table, pages, scales)


def attend_kernel(plan_ref, *refs):
    units, scale_ref = refs[:PARTS], refs[PARTS]
    query_ref, new_ref, cache_ref, scales_ref, att_ref = refs[PARTS + 1 :]
    i = pl.program_id(0)
    span = plan_ref[2, i]
    layers = query_ref.shape[1]
    steps, feats = query_ref.shape[4], query_ref.shape[5]
    heads = feats // 128
    tokens = units[0].shape[3]
    span_max = cache_ref.shape[4]
    rows = heads * steps
    f32 = jnp.float32

    @pl.when(span == 0)
    def _():
        cache_ref[...] = jnp.zeros_like(cache_ref)
        scales_ref[...] = jnp.zeros_like(scales_ref)
        att_ref[...] = jnp.zeros_like(att_ref)

    @pl.when(span > 0)
    def _():
        row = lax.broadcasted_iota(jnp.int32, (rows, 128), 0)
        column = lax.broadcasted_iota(jnp.int32, (rows, 128), 1)
        place = column // 2
        even = column % 2 == 0
        prompt = (column < 2 * span_max) & (place < span)
        fresh = (column >= 2 * span_max) & (place - span_max <= row % steps)
        valid = even & (prompt | fresh)
        own_head = jnp.where(column == row // steps, 1.0, 0.0).astype(jnp.bfloat16)
        block = lax.broadcasted_iota(jnp.int32, (rows, feats), 1) // 128
        block = block == lax.broadcasted_iota(jnp.int32, (rows, feats), 0) // steps
        root = math.sqrt(128)
        spare = 128 - 2 * span_max - 2 * steps
        for l in range(layers):
            for j in range(2):
                for s in range(PARTS):
                    at = 16 * j + tokens * s
                    cache_ref[0, l, 0, 0, at : at + tokens] = units[s][0, l, j]
            scales_ref[0, l, 0, 0] = scale_ref[0, l][:, :, :heads]
            known = cache_ref[0, l, 0, 0].reshape(2 * span_max, feats)
            new = new_ref[0, l, 0, 0].reshape(2 * steps, feats)
            both = jnp.concatenate([known, new, jnp.zeros((spare, feats), known.dtype)], axis=0)
            query = query_ref[0, l, 0, 0].astype(f32)
            query = jnp.concatenate([query] * heads, axis=0)
            query = jnp.where(block, query, 0.0).astype(jnp.bfloat16)
            over = (((1,), (1,)), ((), ()))
            score = lax.dot_general(query, both, over, preferred_element_type=f32)
            scale = [
                jnp.broadcast_to(scale_ref[0, l, j][None], (16, 2, 128)).reshape(32, 128)
                for j in range(2)
            ]
            scale.append(jnp.ones((128 - 2 * span_max, 128), jnp.bfloat16))
            scale = jnp.concatenate(scale, axis=0)
            scale = lax.dot_general(own_head, scale, over, preferred_element_type=f32)
            score = jnp.where(valid, score * scale / root, -jnp.inf)
            top = jnp.max(score, axis=1, keepdims=True)
            power = jnp.exp(score - top)
            total = jnp.sum(power, axis=1, keepdims=True)
            weight = (pltpu.roll(power, 1, axis=1) * scale / total).astype(jnp.bfloat16)
            result = jnp.dot(weight, both, preferred_element_type=f32)
            for h in range(heads):
                part = result[steps * h : steps * h + steps, 128 * h : 128 * h + 128]
                att_ref[0, l, 0, 0, :, 128 * h : 128 * h + 128] = part.astype(att_ref.dtype)


def attend(steps, stores, queries, new_kv):
    layers, nodes, cap, step_count, feats = queries.shape[1:]
    heads = feats // 128
    span_max = 32
    bf16 = jnp.bfloat16

    def unit(shape):
        rest = (0,) * (len(shape) - 1)
        return pl.BlockSpec((1,) + shape[1:], lambda i, p: (p[1, i],) + rest)

    def slot(shape):
        rest = (0,) * (len(shape) - 4)
        return pl.BlockSpec(
            (1, layers, 1, 1) + shape[4:], lambda i, p: (0, 0, i // cap, i % cap) + rest
        )

    outs = [
        (1, layers, nodes, cap, span_max, 2, feats),
        (1, layers, nodes, cap, 2, 2, heads),
        queries.shape,
    ]
    return pl.pallas_call(
        attend_kernel,
        grid_spec=pltpu.PrefetchScalarGridSpec(
            num_scalar_prefetch=1,
            grid=(nodes * cap,),
            in_specs=[unit(s.shape) for s in stores] + [slot(queries.shape), slot(new_kv.shape)],
            out_specs=[slot(s) for s in outs],
        ),
        out_shape=[jax.ShapeDtypeStruct(s, bf16) for s in outs],
        compiler_params=pltpu.CompilerParams(vmem_limit_bytes=40 << 20),
    )(steps, *stores, queries, new_kv)


def slot_ranks(route):
    req_ids = jnp.arange(route.shape[1], dtype=jnp.int32)
    same_dest = route[:, :, None] == route[:, None, :]
    earlier = req_ids[None, :] < req_ids[:, None]
    return jnp.sum((same_dest & earlier[None]).astype(jnp.int32), axis=2)


def padded(prompt_pages, page_scales, page_table, lengths, route, queries, new_kv):
    rep_count = lax.axis_size("rep")
    section_count = lax.axis_size("section")
    head_count = lax.axis_size("head")
    replica = lax.axis_index("rep")
    layers_here = prompt_pages.shape[1]
    pages_here = prompt_pages.shape[2]
    page_rows = prompt_pages.shape[3]
    feature_count = prompt_pages.shape[5]
    heads_total = page_scales.shape[4]
    head_dim = feature_count // heads_total
    group_count = section_count * head_count
    feat_here = feature_count // group_count
    heads_here = heads_total // group_count
    req_count = route.shape[1]
    capacity = max(2, req_count // rep_count)
    pages_each = page_table.shape[1] // req_count
    layer_count = layers_here * section_count
    span_max = page_rows * pages_each
    steps_count = queries.shape[4]
    req_ids = jnp.arange(req_count, dtype=jnp.int32)
    dest_ids = jnp.arange(rep_count, dtype=jnp.int32)
    cap_ids = jnp.arange(capacity, dtype=jnp.int32)
    page_ids = jnp.arange(pages_each, dtype=jnp.int32)
    slot_rank = slot_ranks(route)
    own_route = lax.dynamic_index_in_dim(route, replica, 0, keepdims=False)
    own_rank = lax.dynamic_index_in_dim(slot_rank, replica, 0, keepdims=False)
    send_match = (own_route[None, None, :] == dest_ids[:, None, None]) & (
        own_rank[None, None, :] == cap_ids[None, :, None]
    )
    send_live = jnp.any(send_match, axis=2)
    send_request = jnp.sum(jnp.where(send_match, req_ids[None, None, :], 0), axis=2)
    physical = page_table[0][send_request[:, :, None] * pages_each + page_ids[None, None, :]]
    recv_match = (route[:, None, :] == replica) & (slot_rank[:, None, :] == cap_ids[None, :, None])
    recv_live = jnp.any(recv_match, axis=2)
    slot_span = jnp.sum(jnp.where(recv_match, lengths[:, None, :], 0), axis=2)
    page_view = prompt_pages[0].reshape(
        layers_here, pages_here, page_rows, 2, section_count, head_count, feat_here
    )
    scale_view = page_scales[0].reshape(
        layers_here, pages_here, 1, 2, section_count, head_count, heads_here
    )
    zero_page = jnp.zeros((), prompt_pages.dtype)
    zero_scale = jnp.zeros((), page_scales.dtype)
    regrouped = (
        lax.all_to_all(
            lax.all_to_all(page_view, "section", split_axis=4, concat_axis=0, tiled=True),
            "head",
            split_axis=5,
            concat_axis=1,
            tiled=True,
        ),
        lax.all_to_all(
            lax.all_to_all(scale_view, "section", split_axis=4, concat_axis=0, tiled=True),
            "head",
            split_axis=5,
            concat_axis=1,
            tiled=True,
        ),
    )
    all_pages = regrouped[0].reshape(layer_count, pages_here * head_count, page_rows, 2, feat_here)
    all_scales = regrouped[1].reshape(layer_count, pages_here * head_count, 1, 2, heads_here)
    live_mask = send_live[None, :, :, None, None, None, None]
    slot_pages = jnp.where(live_mask, all_pages[:, physical], zero_page)
    slot_scales = jnp.where(live_mask, all_scales[:, physical], zero_scale)
    received = (
        lax.all_to_all(slot_pages, "rep", split_axis=1, concat_axis=1, tiled=True),
        lax.all_to_all(slot_scales, "rep", split_axis=1, concat_axis=1, tiled=True),
    )
    page_cache = received[0].reshape(layer_count, rep_count, capacity, span_max, 2, feat_here)
    scale_cache = received[1].reshape(layer_count, rep_count, capacity, pages_each, 2, heads_here)
    prompt_keys = page_cache[:, :, :, :, 0, :].reshape(
        layer_count, rep_count, capacity, span_max, heads_here, head_dim
    )
    prompt_values = page_cache[:, :, :, :, 1, :].reshape(
        layer_count, rep_count, capacity, span_max, heads_here, head_dim
    )
    query_rows = queries[0].reshape(
        layer_count, rep_count, capacity, steps_count, heads_here, head_dim
    )
    new_keys = new_kv[0][:, :, :, :, 0, :].reshape(
        layer_count, rep_count, capacity, steps_count, heads_here, head_dim
    )
    new_values = new_kv[0][:, :, :, :, 1, :].reshape(
        layer_count, rep_count, capacity, steps_count, heads_here, head_dim
    )
    score_root = math.sqrt(head_dim)
    key_scale = jnp.transpose(scale_cache[:, :, :, :, 0, :], (0, 1, 2, 4, 3))
    value_scale = jnp.transpose(scale_cache[:, :, :, :, 1, :], (0, 1, 2, 4, 3))
    prompt_dots = jnp.einsum(
        "lrcthd,lrckhd->lrchtk", query_rows, prompt_keys, preferred_element_type=jnp.float32
    )
    prompt_dots = prompt_dots.reshape(
        layer_count, rep_count, capacity, heads_here, steps_count, pages_each, page_rows
    )
    prompt_score = (
        prompt_dots * key_scale[:, :, :, :, None, :, None].astype(jnp.float32) / score_root
    )
    prompt_score = prompt_score.reshape(
        layer_count, rep_count, capacity, heads_here, steps_count, span_max
    )
    fresh_score = (
        jnp.einsum(
            "lrcthd,lrcuhd->lrchtu", query_rows, new_keys, preferred_element_type=jnp.float32
        )
        / score_root
    )
    visible = (jnp.arange(span_max, dtype=jnp.int32)[None, None, :] < slot_span[:, :, None])[
        None, :, :, None, None, :
    ]
    causal = (
        jnp.arange(steps_count, dtype=jnp.int32)[None, :]
        <= jnp.arange(steps_count, dtype=jnp.int32)[:, None]
    )
    row_max = jnp.maximum(
        jnp.max(jnp.where(visible, prompt_score, -jnp.inf), axis=-1, keepdims=True),
        jnp.max(jnp.where(causal, fresh_score, -jnp.inf), axis=-1, keepdims=True),
    )
    exp_prompt = jnp.where(visible, jnp.exp(prompt_score - row_max), 0.0)
    exp_fresh = jnp.where(causal, jnp.exp(fresh_score - row_max), 0.0)
    row_total = jnp.sum(exp_prompt, axis=-1, keepdims=True) + jnp.sum(
        exp_fresh, axis=-1, keepdims=True
    )
    value_weight = jnp.broadcast_to(
        value_scale[:, :, :, :, :, None], value_scale.shape + (page_rows,)
    )
    value_weight = value_weight.reshape(layer_count, rep_count, capacity, heads_here, span_max)[
        :, :, :, :, None, :
    ]
    prompt_weight = (exp_prompt * value_weight.astype(jnp.float32) / row_total).astype(jnp.bfloat16)
    fresh_weight = (exp_fresh / row_total).astype(jnp.bfloat16)
    attended = jnp.einsum(
        "lrchtk,lrckhd->lrcthd", prompt_weight, prompt_values, preferred_element_type=jnp.float32
    )
    attended = attended + jnp.einsum(
        "lrchtu,lrcuhd->lrcthd", fresh_weight, new_values, preferred_element_type=jnp.float32
    )
    attended = jnp.where(recv_live[None, :, :, None, None, None], attended, 0.0).astype(
        jnp.bfloat16
    )
    return (
        page_cache.reshape(1, layer_count, rep_count, capacity, span_max, 2, feat_here),
        scale_cache.reshape(1, layer_count, rep_count, capacity, pages_each, 2, heads_here),
        attended.reshape(1, layer_count, rep_count, capacity, steps_count, feat_here),
    )


def body(prompt_pages, page_scales, page_table, lengths, route, queries, new_kv):
    steps = plan(route, lengths)

    def direct(prompt_pages, page_scales, page_table, lengths, route, queries, new_kv):
        held = page_scales.shape[2]
        scales = page_scales.reshape(held, 2, 16, -1).transpose(2, 0, 1, 3)
        scales = jnp.pad(scales, ((0, 0), (0, 0), (0, 0), (0, 128 - scales.shape[3])))
        stores = exchange(steps, page_table, prompt_pages, scales)
        return tuple(attend(steps, stores, queries, new_kv))

    return lax.cond(
        steps[3, 0] > 0,
        direct,
        padded,
        prompt_pages,
        page_scales,
        page_table,
        lengths,
        route,
        queries,
        new_kv,
    )


def solution(mesh):
    return jax.shard_map(
        body,
        mesh=mesh,
        in_specs=(
            P("rep", "section", "head", None, None, None),
            P("rep", "section", "head", None, None),
            P("rep", None),
            P(),
            P(),
            P("rep", None, None, None, None, ("section", "head")),
            P("rep", None, None, None, None, None, ("section", "head")),
        ),
        out_specs=(
            P("rep", None, None, None, None, None, ("section", "head")),
            P("rep", None, None, None, None, None, ("section", "head")),
            P("rep", None, None, None, None, ("section", "head")),
        ),
        check_vma=False,
    )
```

```python
import math

import jax
import jax.numpy as jnp
import numpy as np
from jax import lax
from jax.experimental import pallas as pl
from jax.experimental.pallas import tpu as pltpu
from jax.sharding import PartitionSpec as P

MESH = pl.DeviceIdType.MESH
NODES = 16
RING = NODES // 2
PORTS = 3
ROUNDS = 16
PARTS = 4
REQS = 8
PAGE = 16
STORE = REQS + PORTS * ROUNDS

ROUTES = (
    0o5555555222222210, 0o5555555222222201, 0o4645121222121045, 0o5555212221210154,
    0o4612132222104545, 0o5531222222015554, 0o2212122210555646, 0o3121222101545455,
    0o1313121055555512, 0o2222210155555451, 0o1312105545565515, 0o2222015455555521,
    0o1310554545561212, 0o2201555555542221, 0o1055555555121212, 0o0155555454222222,
    0o5555552522222210, 0o5555552522222201, 0o5546222322221045, 0o5555522122220154,
    0o4526221222105645, 0o2122312131015554, 0o4323221310464555, 0o2232312101646565,
    0o2222231045454555, 0o3122220155646521, 0o2222105556454623, 0o3131015555542231,
    0o2210455656452312, 0o2101555564555232, 0o1045455546131312, 0o0154546565312122,
)


def links_of(source, dest, code):
    if code == 0:
        return []
    z, y = divmod(source, 2)
    step, mode = (1, (code - 1) % 3) if code <= 3 else (-1, (code - 1) % 3)
    cross = y != dest % 2
    hops = [2] if (cross and mode == 0) or (not cross and mode == 2) else []
    hops += [0 if step > 0 else 1] * (((dest // 2 - z) * step) % RING)
    if (cross and mode != 0) or (not cross and mode == 2):
        hops += [2]
    links = []
    for port in hops:
        links.append((z * 2 + y) * PORTS + port)
        if port == 2:
            y = 1 - y
        else:
            z = (z + (1 if port == 0 else -1)) % RING
    assert z * 2 + y == dest and len(links) < 8
    return links


def path_table():
    table = np.zeros((2, NODES, 8, NODES), np.float32)
    for rank in range(2):
        for source in range(NODES):
            for dest in range(NODES):
                code = (ROUTES[rank * NODES + source] >> (3 * dest)) & 7
                for hop, link in enumerate(links_of(source, dest, code)):
                    table[rank, dest, hop, source] = link + 1
    return table.reshape(2 * NODES * 8, NODES)


def plan_kernel(table_ref, route_ref, length_ref, out_ref, sends, slots, spans):
    f32 = jnp.float32
    lane = lax.broadcasted_iota(jnp.int32, (1, 128), 1)
    source = lane // REQS
    order = lane % REQS
    pick = lax.broadcasted_iota(jnp.int32, (REQS, 128), 1) % REQS
    pick = pick == lax.broadcasted_iota(jnp.int32, (REQS, 128), 0)
    pick = jnp.where(pick, 1.0, 0.0).astype(jnp.bfloat16)

    def flat(ref):
        x = jnp.dot(ref[...].astype(jnp.bfloat16), pick, preferred_element_type=f32)
        x = jnp.where(node == source, x, 0.0)
        return jnp.sum(x, axis=0, keepdims=True)

    node = lax.broadcasted_iota(jnp.int32, (NODES, 128), 0)
    route = flat(route_ref).astype(jnp.int32)
    length = flat(length_ref)
    rank = jnp.zeros_like(route)
    for back in range(1, REQS):
        earlier = pltpu.roll(route, back, axis=1)
        rank = rank + jnp.where((earlier == route) & (order >= back), 1, 0)
    count = jnp.sum(jnp.where(node == route, 1.0, 0.0), axis=1, keepdims=True)
    most = jnp.max(count, axis=0, keepdims=True)
    nodes = lax.broadcasted_iota(jnp.int32, (NODES, 1), 0).astype(f32)
    hot = jnp.min(jnp.where(count == most, nodes, 99.0), axis=0, keepdims=True).astype(jnp.int32)
    hot_z, hot_y = hot // 2, hot % 2

    def relative(x):
        y = x % 2
        return ((x // 2 - hot_z + RING) % RING) * 2 + (y + hot_y - 2 * y * hot_y)

    source_rel, dest_rel = relative(source), relative(route)
    from_one = jnp.where(node == source_rel, 1.0, 0.0).astype(jnp.bfloat16)
    every = jnp.dot(table_ref[...], from_one, preferred_element_type=f32)
    row = lax.broadcasted_iota(jnp.int32, (2 * NODES * 8, 128), 0) // 8
    every = jnp.where(row == rank * NODES + dest_rel, every, 0.0)
    path = every[0:8]
    for i in range(1, 2 * NODES):
        path = path + every[8 * i : 8 * i + 8]
    me = relative(jnp.zeros((1, 1), jnp.int32) + lax.axis_index("rep"))
    me_z, me_y = me // 2, me % 2
    up, down = (me_z + 1) % RING, (me_z + RING - 1) % RING
    to_me = (down * 2 + me_y, up * 2 + me_y, me_z * 2 + 1 - me_y)
    out_link = [(me * PORTS + k + 1).astype(f32) for k in range(PORTS)]
    in_link = [(to_me[k] * PORTS + k + 1).astype(f32) for k in range(PORTS)]
    link = lax.broadcasted_iota(jnp.int32, (NODES * PORTS, 128), 0).astype(f32) + 1.0
    tie = (127 - lane).astype(f32)
    hop_row = lax.broadcasted_iota(jnp.int32, (8, 128), 0)
    held = jnp.where(source_rel == me, order, 0).astype(f32)
    home = dest_rel == me
    own_slot = jnp.where(home, source * 2 + rank, 0).astype(f32)
    own_span = jnp.where(home, length, 0.0)
    for ref in (sends, slots, spans):
        ref[...] = jnp.zeros_like(ref)
    for t in range(ROUNDS):
        now = path[0:1]
        left = jnp.sum(jnp.where(path > 0.0, 1.0, 0.0), axis=0, keepdims=True)
        key = left * 128.0 + tie
        asks = link == now
        first = jnp.max(jnp.where(asks, key, -1.0), axis=1, keepdims=True)
        wins = jnp.where(asks & (first == key), 1.0, 0.0)
        moves = jnp.max(wins, axis=0, keepdims=True) > 0.0
        for k in range(PORTS):
            leaves = moves & (now == out_link[k])
            sends[PORTS * t + k : PORTS * t + k + 1] = jnp.where(leaves, held, 0.0)
        for k in range(PORTS):
            comes = moves & (now == in_link[k])
            held = jnp.where(comes, float(REQS + PORTS * t + k), held)
            slots[PORTS * t + k : PORTS * t + k + 1] = jnp.where(comes, own_slot, 0.0)
            spans[PORTS * t + k : PORTS * t + k + 1] = jnp.where(comes, own_span, 0.0)
        later = jnp.where(hop_row < 7, pltpu.roll(path, 7, axis=0), 0.0)
        path = jnp.where(moves, later, path)
    left = jnp.sum(jnp.where(path > 0.0, 1.0, 0.0), axis=0, keepdims=True)
    stuck = jnp.sum(left, axis=1, keepdims=True)
    square = lax.broadcasted_iota(jnp.int32, (128, 128), 0) == lax.broadcasted_iota(
        jnp.int32, (128, 128), 1
    )

    def lay(rows):
        sums = jnp.sum(rows, axis=1, keepdims=True)
        n = rows.shape[0]
        return jnp.sum(jnp.where(square[:n], sums, 0.0), axis=0, keepdims=True)

    slot = lax.broadcasted_iota(jnp.int32, (2 * NODES, 128), 0)
    mine = (slot == source * 2 + rank) & home
    out = [
        lay(sends[...]),
        lay(jnp.where(mine, held, 0.0)),
        lay(jnp.where(mine, length, 0.0)),
        jnp.where(lane >= 0, jnp.where(stuck > 0.0, 0.0, 1.0), 0.0),
        lay(slots[...]),
        lay(spans[...]),
        jnp.zeros((2, 128), f32),
    ]
    out_ref[...] = jnp.concatenate(out, axis=0).astype(jnp.int32)


def plan(route, lengths):
    return pl.pallas_call(
        plan_kernel,
        out_shape=jax.ShapeDtypeStruct((8, 128), jnp.int32),
        in_specs=[pl.BlockSpec(memory_space=pltpu.VMEM)] * 3,
        out_specs=pl.BlockSpec(memory_space=pltpu.VMEM),
        scratch_shapes=[pltpu.VMEM((128, 128), jnp.float32)] * 3,
    )(jnp.asarray(path_table(), jnp.bfloat16), route, lengths)


def attend(known, new, queries, scale, span):
    f32 = jnp.float32
    bf16 = jnp.bfloat16
    layers = len(known)
    steps, feats = queries[0].shape
    heads = feats // 128
    rows = known[0].shape[0]
    total_rows = rows + new[0].shape[0]
    per_layer = heads * steps
    over = (((1,), (1,)), ((), ()))
    row = lax.broadcasted_iota(jnp.int32, (total_rows, 128), 0)
    lane = lax.broadcasted_iota(jnp.int32, (total_rows, 128), 1)
    even = row % 2 == 0
    part = rows // PARTS
    page = row % part // (part // 2)
    token = PAGE * page + row // part * (PAGE // PARTS) + row % (part // 2) // 2
    fresh = (row >= rows) & ((row - rows) // 2 <= lane % steps)
    valid = even & (((row < rows) & (token < span)) | fresh)
    own_head = lax.broadcasted_iota(jnp.int32, (128, 128), 0)
    own_head = own_head == lax.broadcasted_iota(jnp.int32, (128, 128), 1) // steps
    own_head = jnp.where(own_head, 1.0, 0.0).astype(bf16)
    block = lax.broadcasted_iota(jnp.int32, (per_layer, feats), 1) // 128
    block = block == lax.broadcasted_iota(jnp.int32, (per_layer, feats), 0) // steps

    both = [jnp.concatenate([known[l], new[l]], axis=0) for l in range(layers)]
    query = []
    for one in queries:
        one = jnp.concatenate([one.astype(f32)] * heads, axis=0)
        query.append(jnp.where(block, one, 0.0))
    query.append(jnp.zeros((128 - layers * per_layer, feats), f32))
    query = jnp.concatenate(query, axis=0).astype(bf16)
    score = lax.dot_general(both[0], query, over, preferred_element_type=f32)
    for l in range(1, layers):
        other = lax.dot_general(both[l], query, over, preferred_element_type=f32)
        score = jnp.where(lane // per_layer == l, other, score)
    scale = scale.astype(f32)
    scale = ((scale[0] + scale[1]) + (scale[2] + scale[3])).reshape(4, 128)
    scale = jnp.concatenate([scale, jnp.zeros((12, 128), f32)], axis=0).astype(bf16)
    scale = jnp.dot(scale, own_head, preferred_element_type=f32)
    factor = jnp.where(
        page == 0,
        jnp.where(even, scale[0:1], scale[1:2]),
        jnp.where(even, scale[2:3], scale[3:4]),
    )
    factor = jnp.where(row < rows, factor, 1.0)
    score = jnp.where(valid, score * factor / math.sqrt(128), -jnp.inf)
    power = jnp.exp(score - jnp.max(score, axis=0, keepdims=True))
    total = jnp.sum(power, axis=0, keepdims=True)
    weight = (pltpu.roll(power, 1, axis=0) * factor / total).T
    results = []
    for l in range(layers):
        own = weight[per_layer * l : per_layer * (l + 1)].astype(bf16)
        result = jnp.dot(own, both[l], preferred_element_type=f32)
        parts = [
            result[steps * h : steps * h + steps, 128 * h : 128 * h + 128] for h in range(heads)
        ]
        results.append(jnp.concatenate(parts, axis=1).astype(bf16))
    return results


def exchange_kernel(plan_ref, table_ref, pages, scales, query_hbm, new_hbm, *refs):
    streams = PARTS + 1
    stores = refs[:streams]
    att = refs[streams]
    refs = refs[streams + 1 :]
    groups = refs[:streams]
    lands = refs[streams : 2 * streams]
    packs = refs[2 * streams : 3 * streams]
    queries, news, group_send, group_recv, send_sem, recv_sem, new_sem = refs[3 * streams :]
    rep = lax.axis_index("rep")
    section = lax.axis_index("section")
    head = lax.axis_index("head")
    tokens = groups[0].shape[2]
    held = pages.shape[2]
    feats = groups[0].shape[4]
    layers, _, steps, _ = queries.shape

    peers = []
    for o in range(16):
        peers.append((lax.rem(section + o // 4, 4), lax.rem(head + o % 4, 4)))
    neighbours = (
        lax.rem(rep + 2, NODES),
        lax.rem(rep + NODES - 2, NODES),
        rep + 1 - 2 * lax.rem(rep, 2),
    )
    barrier = pltpu.get_barrier_semaphore()
    for s, h in peers[1:]:
        pl.semaphore_signal(barrier, inc=1, device_id=(rep, s, h), device_id_type=MESH)
    for n in neighbours:
        pl.semaphore_signal(barrier, inc=1, device_id=(n, section, head), device_id_type=MESH)
    pl.semaphore_wait(barrier, 15 + PORTS)

    def block(i, group):
        if i == PARTS:
            return scales.at[group]
        columns = pl.ds(pl.multiple_of(group * feats, 128), feats)
        return pages.at[0, 0, :, pl.ds(tokens * i, tokens), :, columns]

    def place(i, s, h):
        return groups[i].at[s, pl.ds(held * h, held)]

    def regroup(i, o):
        s, h = peers[o]
        return pltpu.make_async_remote_copy(
            src_ref=block(i, s * 4 + h),
            dst_ref=place(i, section, head),
            send_sem=group_send.at[i, o],
            recv_sem=group_recv.at[i, o],
            device_id=(rep, s, h),
            device_id_type=MESH,
        )

    def regroup_own(i):
        return pltpu.make_async_copy(
            block(i, section * 4 + head), place(i, section, head), group_recv.at[i, 0]
        )

    order = [PARTS] + list(range(PARTS))
    for i in order:
        for o in range(1, 16):
            regroup(i, o).start()
        regroup_own(i).start()
    load_query = pltpu.make_async_copy(query_hbm, queries, new_sem.at[0])
    load_new = pltpu.make_async_copy(new_hbm, news, new_sem.at[1])
    load_query.start()
    load_new.start()

    def send(i, slot, k):
        return pltpu.make_async_remote_copy(
            src_ref=packs[i].at[slot, k],
            dst_ref=lands[i].at[slot, k],
            send_sem=send_sem.at[i, slot, k],
            recv_sem=recv_sem.at[i, slot, k],
            device_id=(neighbours[k], section, head),
            device_id_type=MESH,
        )

    def compose(i, t, slot):
        for k in range(PORTS):
            packs[i][slot, k] = stores[i][plan_ref[0, PORTS * t + k]]
        for k in range(PORTS):
            send(i, slot, k).start()

    def arrive(i, t, slot):
        for k in range(PORTS):
            send(i, slot, k).wait_recv()
        for k in range(PORTS):
            stores[i][REQS + PORTS * t + k] = lands[i][slot, k]

    def attend_unit(at, unit, slot, span):
        known = [
            jnp.concatenate(
                [stores[i][unit, l].reshape(4 * tokens, feats) for i in range(PARTS)], axis=0
            )
            for l in range(layers)
        ]
        new = [news[l, slot].reshape(2 * steps, feats) for l in range(layers)]
        query = [queries[l, slot] for l in range(layers)]
        results = attend(known, new, query, stores[PARTS][unit], span)
        for l in range(layers):
            att[at, l] = results[l]

    def attend_own():
        for c in range(2):
            slot = 2 * rep + c
            attend_unit(c, plan_ref[1, slot], slot, plan_ref[2, slot])

    def attend_arrived(t):
        for k in range(PORTS):
            at = PORTS * t + k
            attend_unit(REQS + at, REQS + at, plan_ref[4, at], plan_ref[5, at])

    for i in order:
        regroup_own(i).wait()
        for o in range(1, 16):
            regroup(i, o).wait_recv()
        for q in range(REQS):
            for j in range(2):
                stores[i][q, :, j] = groups[i][:, table_ref[0, 2 * q + j]]
        compose(i, 0, 0)
    load_query.wait()
    load_new.wait()
    attend_own()

    for i in order:
        arrive(i, 0, 0)
        compose(i, 1, 1)
    attend_arrived(0)

    def one(t, carry):
        slot = lax.rem(t, 2)
        for i in order:
            arrive(i, t - 1, 1 - slot)
            for k in range(PORTS):
                send(i, slot, k).wait_send()
            compose(i, t, slot)
        attend_arrived(t - 1)
        return carry

    lax.fori_loop(2, ROUNDS, one, 0)
    for i in order:
        arrive(i, ROUNDS - 1, (ROUNDS - 1) % 2)
    attend_arrived(ROUNDS - 1)
    for i in order:
        for slot in range(2):
            for k in range(PORTS):
                send(i, slot, k).wait_send()
        for o in range(1, 16):
            regroup(i, o).wait_send()


def exchange(steps, page_table, pages, scales, queries, new_kv):
    layers, nodes, cap, step_count, feats = queries.shape[1:]
    held = pages.shape[2]
    tokens = pages.shape[3] // PARTS
    units = [(tokens, 2, feats)] * PARTS + [(2, 128)]
    bf16 = jnp.bfloat16
    anywhere = pl.BlockSpec(memory_space=pl.ANY)
    smem = pl.BlockSpec(memory_space=pltpu.SMEM)
    vmem = pl.BlockSpec(memory_space=pltpu.VMEM)
    scratch = [pltpu.VMEM((layers, 4 * held) + u, bf16) for u in units]
    scratch += [pltpu.VMEM((2, PORTS, layers, 2) + u, bf16) for u in units] * 2
    query_shape = (layers, nodes * cap, step_count, feats)
    new_shape = (layers, nodes * cap, step_count, 2, feats)
    scratch += [pltpu.VMEM(query_shape, bf16), pltpu.VMEM(new_shape, bf16)]
    dma = pltpu.SemaphoreType.DMA
    streams = PARTS + 1
    scratch += [dma((streams, 16)), dma((streams, 16))]
    scratch += [dma((streams, 2, PORTS)), dma((streams, 2, PORTS)), dma((2,))]
    return pl.pallas_call(
        exchange_kernel,
        out_shape=[jax.ShapeDtypeStruct((STORE, layers, 2) + u, bf16) for u in units]
        + [jax.ShapeDtypeStruct((STORE, layers, step_count, feats), bf16)],
        in_specs=[smem, smem] + [anywhere] * 4,
        out_specs=[vmem] * (streams + 1),
        scratch_shapes=scratch,
        compiler_params=pltpu.CompilerParams(
            collective_id=1, has_side_effects=True, vmem_limit_bytes=40 << 20
        ),
        cost_estimate=pl.CostEstimate(flops=0, bytes_accessed=20 << 20, transcendentals=0),
    )(
        steps,
        page_table,
        pages,
        scales,
        queries.reshape(query_shape),
        new_kv.reshape(new_shape),
    )


def place_kernel(plan_ref, *refs):
    units, scales, att = refs[:PARTS], refs[PARTS], refs[PARTS + 1]
    cache_hbm, scales_ref, att_hbm, zero_unit, zero_att, sems = refs[PARTS + 2 :]
    layers, slots, _, _, heads = scales_ref.shape
    tokens = units[0].shape[3]
    cap = 2
    rep = lax.axis_index("rep")
    zero_unit[...] = jnp.zeros_like(zero_unit)
    zero_att[...] = jnp.zeros_like(zero_att)

    def copies(i, live):
        unit = plan_ref[1, i]
        at = jnp.where(i // cap == rep, i % cap, unit)
        out = []
        for s in range(PARTS):
            to = cache_hbm.at[0, :, i // cap, i % cap, :, pl.ds(tokens * s, tokens)]
            source = units[s].at[unit] if live else zero_unit
            out.append(pltpu.make_async_copy(source, to, sems.at[i, s]))
        source = att.at[at] if live else zero_att
        to = att_hbm.at[0, :, i // cap, i % cap]
        return out + [pltpu.make_async_copy(source, to, sems.at[i, PARTS])]

    @pl.loop(0, slots)
    def _(i):
        @pl.when(plan_ref[2, i] > 0)
        def _():
            for copy in copies(i, True):
                copy.start()
            scale = scales[plan_ref[1, i]]
            for l in range(layers):
                scales_ref[l, i] = scale[l][:, :, heads * l : heads * l + heads]

        @pl.when(plan_ref[2, i] == 0)
        def _():
            for copy in copies(i, False):
                copy.start()
            for l in range(layers):
                scales_ref[l, i] = jnp.zeros((2, 2, heads), scales_ref.dtype)

    @pl.loop(0, slots)
    def _(i):
        for copy in copies(i, False):
            copy.wait()


def place(steps, units, queries):
    layers, nodes, cap, step_count, feats = queries.shape[1:]
    heads = feats // 128
    bf16 = jnp.bfloat16
    anywhere = pl.BlockSpec(memory_space=pl.ANY)
    vmem = pl.BlockSpec(memory_space=pltpu.VMEM)
    smem = pl.BlockSpec(memory_space=pltpu.SMEM)
    cache, scales, attention = pl.pallas_call(
        place_kernel,
        in_specs=[smem] + [vmem] * len(units),
        out_specs=[anywhere, vmem, anywhere],
        out_shape=[
            jax.ShapeDtypeStruct((1, layers, nodes, cap, 2, PAGE, 2, feats), bf16),
            jax.ShapeDtypeStruct((layers, nodes * cap, 2, 2, heads), bf16),
            jax.ShapeDtypeStruct(queries.shape, bf16),
        ],
        scratch_shapes=[
            pltpu.VMEM(units[0].shape[1:], bf16),
            pltpu.VMEM(units[PARTS + 1].shape[1:], bf16),
            pltpu.SemaphoreType.DMA((nodes * cap, PARTS + 1)),
        ],
        compiler_params=pltpu.CompilerParams(vmem_limit_bytes=40 << 20),
    )(steps, *units)
    cache = cache.reshape(1, layers, nodes, cap, 2 * PAGE, 2, feats)
    return cache, scales.reshape(1, layers, nodes, cap, 2, 2, heads), attention


def slot_ranks(route):
    req_ids = jnp.arange(route.shape[1], dtype=jnp.int32)
    same_dest = route[:, :, None] == route[:, None, :]
    earlier = req_ids[None, :] < req_ids[:, None]
    return jnp.sum((same_dest & earlier[None]).astype(jnp.int32), axis=2)


def padded(prompt_pages, page_scales, page_table, lengths, route, queries, new_kv):
    rep_count = lax.axis_size("rep")
    section_count = lax.axis_size("section")
    head_count = lax.axis_size("head")
    replica = lax.axis_index("rep")
    layers_here = prompt_pages.shape[1]
    pages_here = prompt_pages.shape[2]
    page_rows = prompt_pages.shape[3]
    feature_count = prompt_pages.shape[5]
    heads_total = page_scales.shape[4]
    head_dim = feature_count // heads_total
    group_count = section_count * head_count
    feat_here = feature_count // group_count
    heads_here = heads_total // group_count
    req_count = route.shape[1]
    capacity = max(2, req_count // rep_count)
    pages_each = page_table.shape[1] // req_count
    layer_count = layers_here * section_count
    span_max = page_rows * pages_each
    steps_count = queries.shape[4]
    req_ids = jnp.arange(req_count, dtype=jnp.int32)
    dest_ids = jnp.arange(rep_count, dtype=jnp.int32)
    cap_ids = jnp.arange(capacity, dtype=jnp.int32)
    page_ids = jnp.arange(pages_each, dtype=jnp.int32)
    slot_rank = slot_ranks(route)
    own_route = lax.dynamic_index_in_dim(route, replica, 0, keepdims=False)
    own_rank = lax.dynamic_index_in_dim(slot_rank, replica, 0, keepdims=False)
    send_match = (own_route[None, None, :] == dest_ids[:, None, None]) & (
        own_rank[None, None, :] == cap_ids[None, :, None]
    )
    send_live = jnp.any(send_match, axis=2)
    send_request = jnp.sum(jnp.where(send_match, req_ids[None, None, :], 0), axis=2)
    physical = page_table[0][send_request[:, :, None] * pages_each + page_ids[None, None, :]]
    recv_match = (route[:, None, :] == replica) & (slot_rank[:, None, :] == cap_ids[None, :, None])
    recv_live = jnp.any(recv_match, axis=2)
    slot_span = jnp.sum(jnp.where(recv_match, lengths[:, None, :], 0), axis=2)
    page_view = prompt_pages[0].reshape(
        layers_here, pages_here, page_rows, 2, section_count, head_count, feat_here
    )
    scale_view = page_scales[0].reshape(
        layers_here, pages_here, 1, 2, section_count, head_count, heads_here
    )
    zero_page = jnp.zeros((), prompt_pages.dtype)
    zero_scale = jnp.zeros((), page_scales.dtype)
    regrouped = (
        lax.all_to_all(
            lax.all_to_all(page_view, "section", split_axis=4, concat_axis=0, tiled=True),
            "head",
            split_axis=5,
            concat_axis=1,
            tiled=True,
        ),
        lax.all_to_all(
            lax.all_to_all(scale_view, "section", split_axis=4, concat_axis=0, tiled=True),
            "head",
            split_axis=5,
            concat_axis=1,
            tiled=True,
        ),
    )
    all_pages = regrouped[0].reshape(layer_count, pages_here * head_count, page_rows, 2, feat_here)
    all_scales = regrouped[1].reshape(layer_count, pages_here * head_count, 1, 2, heads_here)
    live_mask = send_live[None, :, :, None, None, None, None]
    slot_pages = jnp.where(live_mask, all_pages[:, physical], zero_page)
    slot_scales = jnp.where(live_mask, all_scales[:, physical], zero_scale)
    received = (
        lax.all_to_all(slot_pages, "rep", split_axis=1, concat_axis=1, tiled=True),
        lax.all_to_all(slot_scales, "rep", split_axis=1, concat_axis=1, tiled=True),
    )
    page_cache = received[0].reshape(layer_count, rep_count, capacity, span_max, 2, feat_here)
    scale_cache = received[1].reshape(layer_count, rep_count, capacity, pages_each, 2, heads_here)
    prompt_keys = page_cache[:, :, :, :, 0, :].reshape(
        layer_count, rep_count, capacity, span_max, heads_here, head_dim
    )
    prompt_values = page_cache[:, :, :, :, 1, :].reshape(
        layer_count, rep_count, capacity, span_max, heads_here, head_dim
    )
    query_rows = queries[0].reshape(
        layer_count, rep_count, capacity, steps_count, heads_here, head_dim
    )
    new_keys = new_kv[0][:, :, :, :, 0, :].reshape(
        layer_count, rep_count, capacity, steps_count, heads_here, head_dim
    )
    new_values = new_kv[0][:, :, :, :, 1, :].reshape(
        layer_count, rep_count, capacity, steps_count, heads_here, head_dim
    )
    score_root = math.sqrt(head_dim)
    key_scale = jnp.transpose(scale_cache[:, :, :, :, 0, :], (0, 1, 2, 4, 3))
    value_scale = jnp.transpose(scale_cache[:, :, :, :, 1, :], (0, 1, 2, 4, 3))
    prompt_dots = jnp.einsum(
        "lrcthd,lrckhd->lrchtk", query_rows, prompt_keys, preferred_element_type=jnp.float32
    )
    prompt_dots = prompt_dots.reshape(
        layer_count, rep_count, capacity, heads_here, steps_count, pages_each, page_rows
    )
    prompt_score = (
        prompt_dots * key_scale[:, :, :, :, None, :, None].astype(jnp.float32) / score_root
    )
    prompt_score = prompt_score.reshape(
        layer_count, rep_count, capacity, heads_here, steps_count, span_max
    )
    fresh_score = (
        jnp.einsum(
            "lrcthd,lrcuhd->lrchtu", query_rows, new_keys, preferred_element_type=jnp.float32
        )
        / score_root
    )
    visible = (jnp.arange(span_max, dtype=jnp.int32)[None, None, :] < slot_span[:, :, None])[
        None, :, :, None, None, :
    ]
    causal = (
        jnp.arange(steps_count, dtype=jnp.int32)[None, :]
        <= jnp.arange(steps_count, dtype=jnp.int32)[:, None]
    )
    row_max = jnp.maximum(
        jnp.max(jnp.where(visible, prompt_score, -jnp.inf), axis=-1, keepdims=True),
        jnp.max(jnp.where(causal, fresh_score, -jnp.inf), axis=-1, keepdims=True),
    )
    exp_prompt = jnp.where(visible, jnp.exp(prompt_score - row_max), 0.0)
    exp_fresh = jnp.where(causal, jnp.exp(fresh_score - row_max), 0.0)
    row_total = jnp.sum(exp_prompt, axis=-1, keepdims=True) + jnp.sum(
        exp_fresh, axis=-1, keepdims=True
    )
    value_weight = jnp.broadcast_to(
        value_scale[:, :, :, :, :, None], value_scale.shape + (page_rows,)
    )
    value_weight = value_weight.reshape(layer_count, rep_count, capacity, heads_here, span_max)[
        :, :, :, :, None, :
    ]
    prompt_weight = (exp_prompt * value_weight.astype(jnp.float32) / row_total).astype(jnp.bfloat16)
    fresh_weight = (exp_fresh / row_total).astype(jnp.bfloat16)
    attended = jnp.einsum(
        "lrchtk,lrckhd->lrcthd", prompt_weight, prompt_values, preferred_element_type=jnp.float32
    )
    attended = attended + jnp.einsum(
        "lrchtu,lrcuhd->lrcthd", fresh_weight, new_values, preferred_element_type=jnp.float32
    )
    attended = jnp.where(recv_live[None, :, :, None, None, None], attended, 0.0).astype(
        jnp.bfloat16
    )
    return (
        page_cache.reshape(1, layer_count, rep_count, capacity, span_max, 2, feat_here),
        scale_cache.reshape(1, layer_count, rep_count, capacity, pages_each, 2, heads_here),
        attended.reshape(1, layer_count, rep_count, capacity, steps_count, feat_here),
    )


def body(prompt_pages, page_scales, page_table, lengths, route, queries, new_kv):
    steps = plan(route, lengths)

    def direct(prompt_pages, page_scales, page_table, lengths, route, queries, new_kv):
        held = page_scales.shape[2]
        scales = page_scales.reshape(held, 2, 16, -1).transpose(2, 0, 1, 3)
        heads = scales.shape[3]
        scales = jnp.pad(jnp.tile(scales, (1, 1, 1, 4)), ((0, 0),) * 3 + ((0, 128 - 4 * heads),))
        own = jnp.arange(128) // heads == lax.axis_index("section")
        scales = jnp.where(own, scales, jnp.zeros((), scales.dtype))
        units = exchange(steps, page_table, prompt_pages, scales, queries, new_kv)
        return tuple(place(steps, units, queries))

    return lax.cond(
        steps[3, 0] > 0,
        direct,
        padded,
        prompt_pages,
        page_scales,
        page_table,
        lengths,
        route,
        queries,
        new_kv,
    )


def solution(mesh):
    return jax.shard_map(
        body,
        mesh=mesh,
        in_specs=(
            P("rep", "section", "head", None, None, None),
            P("rep", "section", "head", None, None),
            P("rep", None),
            P(),
            P(),
            P("rep", None, None, None, None, ("section", "head")),
            P("rep", None, None, None, None, None, ("section", "head")),
        ),
        out_specs=(
            P("rep", None, None, None, None, None, ("section", "head")),
            P("rep", None, None, None, None, None, ("section", "head")),
            P("rep", None, None, None, None, ("section", "head")),
        ),
        check_vma=False,
    )
```

```python
import functools
import math

import jax
import jax.numpy as jnp
import numpy as np
from jax import lax
from jax.experimental import pallas as pl
from jax.experimental.pallas import tpu as pltpu
from jax.sharding import PartitionSpec as P

MESH = pl.DeviceIdType.MESH
NODES = 16
RING = NODES // 2
PORTS = 3
TIERS = (13, 14, 16)
ROUNDS = TIERS[-1]
PARTS = 4
REQS = 8
PAGE = 16
OFFSETS = (0, 0, 0, 0)

ROUTES = (
    0o5555555222222210, 0o5555555222222201, 0o4645121222121045, 0o5555212221210154,
    0o4612132222104545, 0o5531222222015554, 0o2212122210555646, 0o3121222101545455,
    0o1313121055555512, 0o2222210155555451, 0o1312105545565515, 0o2222015455555521,
    0o1310554545561212, 0o2201555555542221, 0o1055555555121212, 0o0155555454222222,
    0o5555552522222210, 0o5555552522222201, 0o5546222322221045, 0o5555522122220154,
    0o4526221222105645, 0o2122312131015554, 0o4323221310464555, 0o2232312101646565,
    0o2222231045454555, 0o3122220155646521, 0o2222105556454623, 0o3131015555542231,
    0o2210455656452312, 0o2101555564555232, 0o1045455546131312, 0o0154546565312122,
)


def links_of(source, dest, code):
    if code == 0:
        return []
    z, y = divmod(source, 2)
    step, mode = (1, (code - 1) % 3) if code <= 3 else (-1, (code - 1) % 3)
    cross = y != dest % 2
    hops = [2] if (cross and mode == 0) or (not cross and mode == 2) else []
    hops += [0 if step > 0 else 1] * (((dest // 2 - z) * step) % RING)
    if (cross and mode != 0) or (not cross and mode == 2):
        hops += [2]
    links = []
    for port in hops:
        links.append((z * 2 + y) * PORTS + port)
        if port == 2:
            y = 1 - y
        else:
            z = (z + (1 if port == 0 else -1)) % RING
    assert z * 2 + y == dest and len(links) < 8
    return links


def path_table():
    table = np.zeros((2, NODES, 8, NODES), np.float32)
    for rank in range(2):
        for source in range(NODES):
            for dest in range(NODES):
                code = (ROUTES[rank * NODES + source] >> (3 * dest)) & 7
                for hop, link in enumerate(links_of(source, dest, code)):
                    table[rank, dest, hop, source] = link + 1
    return table.reshape(2 * NODES * 8, NODES)


def plan_kernel(table_ref, inputs_ref, out_ref, sends, slots, spans):
    f32 = jnp.float32
    lane = lax.broadcasted_iota(jnp.int32, (1, 128), 1)
    source = lane // REQS
    order = lane % REQS
    pick = lax.broadcasted_iota(jnp.int32, (REQS, 128), 1) % REQS
    pick = pick == lax.broadcasted_iota(jnp.int32, (REQS, 128), 0)
    pick = jnp.where(pick, 1.0, 0.0).astype(jnp.bfloat16)

    def flat(ref):
        x = jnp.dot(ref.astype(jnp.bfloat16), pick, preferred_element_type=f32)
        x = jnp.where(node == source, x, 0.0)
        return jnp.sum(x, axis=0, keepdims=True)

    node = lax.broadcasted_iota(jnp.int32, (NODES, 128), 0)
    route = flat(inputs_ref[:NODES]).astype(jnp.int32)
    length = flat(inputs_ref[NODES:])
    rank = jnp.zeros_like(route)
    for back in range(1, REQS):
        earlier = pltpu.roll(route, back, axis=1)
        rank = rank + jnp.where((earlier == route) & (order >= back), 1, 0)
    count = jnp.sum(jnp.where(node == route, 1.0, 0.0), axis=1, keepdims=True)
    most = jnp.max(count, axis=0, keepdims=True)
    nodes = lax.broadcasted_iota(jnp.int32, (NODES, 1), 0).astype(f32)
    hot = jnp.min(jnp.where(count == most, nodes, 99.0), axis=0, keepdims=True).astype(jnp.int32)
    hot_z, hot_y = hot // 2, hot % 2

    def relative(x):
        y = x % 2
        return ((x // 2 - hot_z + RING) % RING) * 2 + (y + hot_y - 2 * y * hot_y)

    source_rel, dest_rel = relative(source), relative(route)
    from_one = jnp.where(node == source_rel, 1.0, 0.0).astype(jnp.bfloat16)
    every = jnp.dot(table_ref[...], from_one, preferred_element_type=f32)
    row = lax.broadcasted_iota(jnp.int32, (2 * NODES * 8, 128), 0) // 8
    every = jnp.where(row == rank * NODES + dest_rel, every, 0.0)
    path = every[0:8]
    for i in range(1, 2 * NODES):
        path = path + every[8 * i : 8 * i + 8]
    me = relative(jnp.zeros((1, 1), jnp.int32) + lax.axis_index("rep"))
    me_z, me_y = me // 2, me % 2
    up, down = (me_z + 1) % RING, (me_z + RING - 1) % RING
    to_me = (down * 2 + me_y, up * 2 + me_y, me_z * 2 + 1 - me_y)
    out_link = [(me * PORTS + k + 1).astype(f32) for k in range(PORTS)]
    in_link = [(to_me[k] * PORTS + k + 1).astype(f32) for k in range(PORTS)]
    link = lax.broadcasted_iota(jnp.int32, (NODES * PORTS, 128), 0).astype(f32) + 1.0
    tie = (127 - lane).astype(f32)
    hop_row = lax.broadcasted_iota(jnp.int32, (8, 128), 0)
    held = jnp.where(source_rel == me, order, 0).astype(f32)
    home = dest_rel == me
    own_slot = jnp.where(home, source * 2 + rank, 0).astype(f32)
    own_span = jnp.where(home, length, 0.0)
    for ref in (sends, slots, spans):
        ref[...] = jnp.zeros_like(ref)
    fine = []
    for t in range(ROUNDS):
        now = path[0:1]
        if t in TIERS:
            fine.append(jnp.max(now, axis=1, keepdims=True) == 0.0)
        left = jnp.sum(jnp.where(path > 0.0, 1.0, 0.0), axis=0, keepdims=True)
        key = left * 128.0 + tie
        asks = link == now
        first = jnp.max(jnp.where(asks, key, -1.0), axis=1, keepdims=True)
        wins = jnp.where(asks & (first == key), 1.0, 0.0)
        moves = jnp.max(wins, axis=0, keepdims=True) > 0.0
        for k in range(PORTS):
            leaves = moves & (now == out_link[k])
            sends[PORTS * t + k : PORTS * t + k + 1] = jnp.where(leaves, held, 0.0)
        for k in range(PORTS):
            comes = moves & (now == in_link[k])
            held = jnp.where(comes, float(REQS + PORTS * t + k), held)
            slots[PORTS * t + k : PORTS * t + k + 1] = jnp.where(comes, own_slot, 0.0)
            spans[PORTS * t + k : PORTS * t + k + 1] = jnp.where(comes, own_span, 0.0)
        later = jnp.where(hop_row < 7, pltpu.roll(path, 7, axis=0), 0.0)
        path = jnp.where(moves, later, path)
    fine.append(jnp.max(path[0:1], axis=1, keepdims=True) == 0.0)
    tier = sum(jnp.where(done, 0.0, 1.0) for done in fine)
    square = lax.broadcasted_iota(jnp.int32, (128, 128), 0) == lax.broadcasted_iota(
        jnp.int32, (128, 128), 1
    )

    def lay(rows):
        sums = jnp.sum(rows, axis=1, keepdims=True)
        n = rows.shape[0]
        return jnp.sum(jnp.where(square[:n], sums, 0.0), axis=0, keepdims=True)

    slot = lax.broadcasted_iota(jnp.int32, (2 * NODES, 128), 0)
    mine = (slot == source * 2 + rank) & home
    out = [
        lay(sends[...]),
        lay(jnp.where(mine, held, 0.0)),
        lay(jnp.where(mine, length, 0.0)),
        jnp.where(lane >= 0, tier, 0.0),
        lay(slots[...]),
        lay(spans[...]),
        jnp.zeros((2, 128), f32),
    ]
    out_ref[...] = jnp.concatenate(out, axis=0).astype(jnp.int32)


def plan(route, lengths):
    return pl.pallas_call(
        plan_kernel,
        out_shape=jax.ShapeDtypeStruct((8, 128), jnp.int32),
        in_specs=[pl.BlockSpec(memory_space=pltpu.VMEM)] * 2,
        out_specs=pl.BlockSpec(memory_space=pltpu.VMEM),
        scratch_shapes=[pltpu.VMEM((128, 128), jnp.float32)] * 3,
    )(jnp.asarray(path_table(), jnp.bfloat16), jnp.concatenate([route, lengths], axis=0))


def attend(known, new, queries, scale, span):
    f32 = jnp.float32
    bf16 = jnp.bfloat16
    layers = len(known)
    steps, feats = queries[0].shape
    heads = feats // 128
    rows = known[0].shape[0]
    total_rows = rows + new[0].shape[0]
    per_layer = heads * steps
    over = (((1,), (1,)), ((), ()))
    row = lax.broadcasted_iota(jnp.int32, (total_rows, 128), 0)
    lane = lax.broadcasted_iota(jnp.int32, (total_rows, 128), 1)
    even = row % 2 == 0
    part = rows // PARTS
    page = row % part // (part // 2)
    token = PAGE * page + row // part * (PAGE // PARTS) + row % (part // 2) // 2
    fresh = (row >= rows) & ((row - rows) // 2 <= lane % steps)
    valid = even & (((row < rows) & (token < span)) | fresh)
    own_head = lax.broadcasted_iota(jnp.int32, (128, 128), 0)
    own_head = own_head == lax.broadcasted_iota(jnp.int32, (128, 128), 1) // steps
    own_head = jnp.where(own_head, 1.0, 0.0).astype(bf16)
    block = lax.broadcasted_iota(jnp.int32, (per_layer, feats), 1) // 128
    block = block == lax.broadcasted_iota(jnp.int32, (per_layer, feats), 0) // steps

    both = [jnp.concatenate([known[l], new[l]], axis=0) for l in range(layers)]
    query = []
    for one in queries:
        one = jnp.concatenate([one.astype(f32)] * heads, axis=0)
        query.append(jnp.where(block, one, 0.0))
    query.append(jnp.zeros((128 - layers * per_layer, feats), f32))
    query = jnp.concatenate(query, axis=0).astype(bf16)
    score = lax.dot_general(both[0], query, over, preferred_element_type=f32)
    for l in range(1, layers):
        other = lax.dot_general(both[l], query, over, preferred_element_type=f32)
        score = jnp.where(lane // per_layer == l, other, score)
    scale = scale.astype(f32)
    scale = ((scale[0] + scale[1]) + (scale[2] + scale[3])).reshape(4, 128)
    scale = jnp.concatenate([scale, jnp.zeros((12, 128), f32)], axis=0).astype(bf16)
    scale = jnp.dot(scale, own_head, preferred_element_type=f32)
    factor = jnp.where(
        page == 0,
        jnp.where(even, scale[0:1], scale[1:2]),
        jnp.where(even, scale[2:3], scale[3:4]),
    )
    factor = jnp.where(row < rows, factor, 1.0)
    score = jnp.where(valid, score * factor / math.sqrt(128), -jnp.inf)
    power = jnp.exp(score - jnp.max(score, axis=0, keepdims=True))
    total = jnp.sum(power, axis=0, keepdims=True)
    weight = (pltpu.roll(power, 1, axis=0) * factor / total).T
    results = []
    for l in range(layers):
        own = weight[per_layer * l : per_layer * (l + 1)].astype(bf16)
        result = jnp.dot(own, both[l], preferred_element_type=f32)
        parts = [
            result[steps * h : steps * h + steps, 128 * h : 128 * h + 128] for h in range(heads)
        ]
        results.append(jnp.concatenate(parts, axis=1).astype(bf16))
    return results


def exchange_kernel(rounds, plan_ref, table_ref, pages, scales, query_hbm, new_hbm, *refs):
    streams = PARTS + 1
    stores = refs[:streams]
    att = refs[streams]
    refs = refs[streams + 1 :]
    groups = refs[:streams]
    lands = refs[streams : 2 * streams]
    packs = refs[2 * streams : 3 * streams]
    queries, news, group_send, group_recv, send_sem, recv_sem, new_sem = refs[3 * streams :]
    rep = lax.axis_index("rep")
    section = lax.axis_index("section")
    head = lax.axis_index("head")
    tokens = groups[0].shape[2]
    held = pages.shape[2]
    feats = groups[0].shape[4]
    layers, _, steps, _ = queries.shape

    peers = []
    for o in range(16):
        peers.append((lax.rem(section + o // 4, 4), lax.rem(head + o % 4, 4)))
    neighbours = (
        lax.rem(rep + 2, NODES),
        lax.rem(rep + NODES - 2, NODES),
        rep + 1 - 2 * lax.rem(rep, 2),
    )
    barrier = pltpu.get_barrier_semaphore()
    for s, h in peers[1:]:
        pl.semaphore_signal(barrier, inc=1, device_id=(rep, s, h), device_id_type=MESH)
    for n in neighbours:
        pl.semaphore_signal(barrier, inc=1, device_id=(n, section, head), device_id_type=MESH)
    pl.semaphore_wait(barrier, 15 + PORTS)

    def block(i, group):
        if i == PARTS:
            return scales.at[group]
        columns = pl.ds(pl.multiple_of(group * feats, 128), feats)
        return pages.at[0, 0, :, pl.ds(tokens * i, tokens), :, columns]

    def place(i, s, h):
        return groups[i].at[s, pl.ds(held * h, held)]

    def regroup(i, o):
        s, h = peers[o]
        return pltpu.make_async_remote_copy(
            src_ref=block(i, s * 4 + h),
            dst_ref=place(i, section, head),
            send_sem=group_send.at[i, o],
            recv_sem=group_recv.at[i, o],
            device_id=(rep, s, h),
            device_id_type=MESH,
        )

    def regroup_own(i):
        return pltpu.make_async_copy(
            block(i, section * 4 + head), place(i, section, head), group_recv.at[i, 0]
        )

    order = [PARTS] + list(range(PARTS))
    for i in order:
        for o in range(1, 16):
            regroup(i, o).start()
        regroup_own(i).start()
    load_query = pltpu.make_async_copy(query_hbm, queries, new_sem.at[0])
    load_new = pltpu.make_async_copy(new_hbm, news, new_sem.at[1])
    load_query.start()
    load_new.start()

    def send(i, slot, k):
        return pltpu.make_async_remote_copy(
            src_ref=packs[i].at[slot, k],
            dst_ref=lands[i].at[slot, k],
            send_sem=send_sem.at[i, slot, k],
            recv_sem=recv_sem.at[i, slot, k],
            device_id=(neighbours[k], section, head),
            device_id_type=MESH,
        )

    def compose(i, t, slot):
        for k in range(PORTS):
            packs[i][slot, k] = stores[i][plan_ref[0, PORTS * t + k]]
        for k in range(PORTS):
            send(i, slot, k).start()

    def arrive(i, t, slot):
        for k in range(PORTS):
            send(i, slot, k).wait_recv()
        for k in range(PORTS):
            stores[i][REQS + PORTS * t + k] = lands[i][slot, k]

    def attend_unit(at, unit, slot, span):
        known = [
            jnp.concatenate(
                [stores[i][unit, l].reshape(4 * tokens, feats) for i in range(PARTS)], axis=0
            )
            for l in range(layers)
        ]
        new = [news[l, slot].reshape(2 * steps, feats) for l in range(layers)]
        query = [queries[l, slot] for l in range(layers)]
        results = attend(known, new, query, stores[PARTS][unit], span)
        for l in range(layers):
            att[at, l] = results[l]

    def attend_own():
        for c in range(2):
            slot = 2 * rep + c
            attend_unit(c, plan_ref[1, slot], slot, plan_ref[2, slot])

    def attend_arrived(t):
        for k in range(PORTS):
            at = PORTS * t + k
            attend_unit(REQS + at, REQS + at, plan_ref[4, at], plan_ref[5, at])

    lag = OFFSETS + (0,)
    most = max(lag)

    def first(i):
        regroup_own(i).wait()
        for o in range(1, 16):
            regroup(i, o).wait_recv()
        for q in range(REQS):
            for j in range(2):
                stores[i][q, :, j] = groups[i][:, table_ref[0, 2 * q + j]]
        compose(i, 0, 0)

    def attend_at(time, k):
        if isinstance(time, int) and not 0 < time - most <= rounds:
            return
        at = PORTS * (time - most - 1) + k
        attend_unit(REQS + at, REQS + at, plan_ref[4, at], plan_ref[5, at])

    def beat(time):
        for n, i in enumerate(order):
            t = time - lag[i]
            if not isinstance(time, int):
                slot = lax.rem(t, 2)
                arrive(i, t - 1, 1 - slot)
                for k in range(PORTS):
                    send(i, slot, k).wait_send()
                compose(i, t, slot)
            elif t == 0:
                first(i)
            elif 0 < t <= rounds:
                arrive(i, t - 1, (t - 1) % 2)
                if t >= 2 and t < rounds:
                    for k in range(PORTS):
                        send(i, t % 2, k).wait_send()
                if t < rounds:
                    compose(i, t, t % 2)
            if n == PARTS:
                for k in range(PORTS):
                    attend_at(time, k)

    for time in range(most + 2):
        beat(time)
        if time == most:
            load_query.wait()
            load_new.wait()
            attend_own()

    def one(time, carry):
        beat(time)
        return carry

    lax.fori_loop(most + 2, rounds, one, 0)
    for time in range(rounds, rounds + most + 2):
        beat(time)
    for i in order:
        for slot in range(2):
            for k in range(PORTS):
                send(i, slot, k).wait_send()
        for o in range(1, 16):
            regroup(i, o).wait_send()


def exchange(rounds, steps, page_table, pages, scales, queries, new_kv):
    layers, nodes, cap, step_count, feats = queries.shape[1:]
    held = pages.shape[2]
    tokens = pages.shape[3] // PARTS
    store = REQS + PORTS * rounds
    units = [(tokens, 2, feats)] * PARTS + [(2, 128)]
    bf16 = jnp.bfloat16
    anywhere = pl.BlockSpec(memory_space=pl.ANY)
    smem = pl.BlockSpec(memory_space=pltpu.SMEM)
    vmem = pl.BlockSpec(memory_space=pltpu.VMEM)
    scratch = [pltpu.VMEM((layers, 4 * held) + u, bf16) for u in units]
    scratch += [pltpu.VMEM((2, PORTS, layers, 2) + u, bf16) for u in units] * 2
    query_shape = (layers, nodes * cap, step_count, feats)
    new_shape = (layers, nodes * cap, step_count, 2, feats)
    scratch += [pltpu.VMEM(query_shape, bf16), pltpu.VMEM(new_shape, bf16)]
    dma = pltpu.SemaphoreType.DMA
    streams = PARTS + 1
    scratch += [dma((streams, 16)), dma((streams, 16))]
    scratch += [dma((streams, 2, PORTS)), dma((streams, 2, PORTS)), dma((2,))]
    return pl.pallas_call(
        functools.partial(exchange_kernel, rounds),
        out_shape=[jax.ShapeDtypeStruct((store, layers, 2) + u, bf16) for u in units]
        + [jax.ShapeDtypeStruct((store, layers, step_count, feats), bf16)],
        in_specs=[smem, smem] + [anywhere] * 4,
        out_specs=[vmem] * (streams + 1),
        scratch_shapes=scratch,
        compiler_params=pltpu.CompilerParams(
            collective_id=rounds, has_side_effects=True, vmem_limit_bytes=40 << 20
        ),
        cost_estimate=pl.CostEstimate(flops=0, bytes_accessed=20 << 20, transcendentals=0),
    )(
        steps,
        page_table,
        pages,
        scales,
        queries.reshape(query_shape),
        new_kv.reshape(new_shape),
    )


def place_kernel(plan_ref, *refs):
    units, scales, att = refs[:PARTS], refs[PARTS], refs[PARTS + 1]
    cache_hbm, scales_ref, att_hbm, zero_unit, zero_att, sems = refs[PARTS + 2 :]
    layers, slots, _, _, heads = scales_ref.shape
    tokens = units[0].shape[3]
    cap = 2
    rep = lax.axis_index("rep")
    zero_unit[...] = jnp.zeros_like(zero_unit)
    zero_att[...] = jnp.zeros_like(zero_att)

    def copies(i, live):
        unit = plan_ref[1, i]
        at = jnp.where(i // cap == rep, i % cap, unit)
        out = []
        for s in range(PARTS):
            to = cache_hbm.at[0, :, i // cap, i % cap, :, pl.ds(tokens * s, tokens)]
            source = units[s].at[unit] if live else zero_unit
            out.append(pltpu.make_async_copy(source, to, sems.at[i, s]))
        source = att.at[at] if live else zero_att
        to = att_hbm.at[0, :, i // cap, i % cap]
        return out + [pltpu.make_async_copy(source, to, sems.at[i, PARTS])]

    @pl.loop(0, slots)
    def _(i):
        @pl.when(plan_ref[2, i] > 0)
        def _():
            for copy in copies(i, True):
                copy.start()
            scale = scales[plan_ref[1, i]]
            for l in range(layers):
                scales_ref[l, i] = scale[l][:, :, heads * l : heads * l + heads]

        @pl.when(plan_ref[2, i] == 0)
        def _():
            for copy in copies(i, False):
                copy.start()
            for l in range(layers):
                scales_ref[l, i] = jnp.zeros((2, 2, heads), scales_ref.dtype)

    @pl.loop(0, slots)
    def _(i):
        for copy in copies(i, False):
            copy.wait()


def place(steps, units, queries):
    layers, nodes, cap, step_count, feats = queries.shape[1:]
    heads = feats // 128
    bf16 = jnp.bfloat16
    anywhere = pl.BlockSpec(memory_space=pl.ANY)
    vmem = pl.BlockSpec(memory_space=pltpu.VMEM)
    smem = pl.BlockSpec(memory_space=pltpu.SMEM)
    cache, scales, attention = pl.pallas_call(
        place_kernel,
        in_specs=[smem] + [vmem] * len(units),
        out_specs=[anywhere, vmem, anywhere],
        out_shape=[
            jax.ShapeDtypeStruct((1, layers, nodes, cap, 2, PAGE, 2, feats), bf16),
            jax.ShapeDtypeStruct((layers, nodes * cap, 2, 2, heads), bf16),
            jax.ShapeDtypeStruct(queries.shape, bf16),
        ],
        scratch_shapes=[
            pltpu.VMEM(units[0].shape[1:], bf16),
            pltpu.VMEM(units[PARTS + 1].shape[1:], bf16),
            pltpu.SemaphoreType.DMA((nodes * cap, PARTS + 1)),
        ],
        compiler_params=pltpu.CompilerParams(vmem_limit_bytes=40 << 20),
    )(steps, *units)
    cache = cache.reshape(1, layers, nodes, cap, 2 * PAGE, 2, feats)
    return cache, scales.reshape(1, layers, nodes, cap, 2, 2, heads), attention


def slot_ranks(route):
    req_ids = jnp.arange(route.shape[1], dtype=jnp.int32)
    same_dest = route[:, :, None] == route[:, None, :]
    earlier = req_ids[None, :] < req_ids[:, None]
    return jnp.sum((same_dest & earlier[None]).astype(jnp.int32), axis=2)


def padded(prompt_pages, page_scales, page_table, lengths, route, queries, new_kv):
    rep_count = lax.axis_size("rep")
    section_count = lax.axis_size("section")
    head_count = lax.axis_size("head")
    replica = lax.axis_index("rep")
    layers_here = prompt_pages.shape[1]
    pages_here = prompt_pages.shape[2]
    page_rows = prompt_pages.shape[3]
    feature_count = prompt_pages.shape[5]
    heads_total = page_scales.shape[4]
    head_dim = feature_count // heads_total
    group_count = section_count * head_count
    feat_here = feature_count // group_count
    heads_here = heads_total // group_count
    req_count = route.shape[1]
    capacity = max(2, req_count // rep_count)
    pages_each = page_table.shape[1] // req_count
    layer_count = layers_here * section_count
    span_max = page_rows * pages_each
    steps_count = queries.shape[4]
    req_ids = jnp.arange(req_count, dtype=jnp.int32)
    dest_ids = jnp.arange(rep_count, dtype=jnp.int32)
    cap_ids = jnp.arange(capacity, dtype=jnp.int32)
    page_ids = jnp.arange(pages_each, dtype=jnp.int32)
    slot_rank = slot_ranks(route)
    own_route = lax.dynamic_index_in_dim(route, replica, 0, keepdims=False)
    own_rank = lax.dynamic_index_in_dim(slot_rank, replica, 0, keepdims=False)
    send_match = (own_route[None, None, :] == dest_ids[:, None, None]) & (
        own_rank[None, None, :] == cap_ids[None, :, None]
    )
    send_live = jnp.any(send_match, axis=2)
    send_request = jnp.sum(jnp.where(send_match, req_ids[None, None, :], 0), axis=2)
    physical = page_table[0][send_request[:, :, None] * pages_each + page_ids[None, None, :]]
    recv_match = (route[:, None, :] == replica) & (slot_rank[:, None, :] == cap_ids[None, :, None])
    recv_live = jnp.any(recv_match, axis=2)
    slot_span = jnp.sum(jnp.where(recv_match, lengths[:, None, :], 0), axis=2)
    page_view = prompt_pages[0].reshape(
        layers_here, pages_here, page_rows, 2, section_count, head_count, feat_here
    )
    scale_view = page_scales[0].reshape(
        layers_here, pages_here, 1, 2, section_count, head_count, heads_here
    )
    zero_page = jnp.zeros((), prompt_pages.dtype)
    zero_scale = jnp.zeros((), page_scales.dtype)
    regrouped = (
        lax.all_to_all(
            lax.all_to_all(page_view, "section", split_axis=4, concat_axis=0, tiled=True),
            "head",
            split_axis=5,
            concat_axis=1,
            tiled=True,
        ),
        lax.all_to_all(
            lax.all_to_all(scale_view, "section", split_axis=4, concat_axis=0, tiled=True),
            "head",
            split_axis=5,
            concat_axis=1,
            tiled=True,
        ),
    )
    all_pages = regrouped[0].reshape(layer_count, pages_here * head_count, page_rows, 2, feat_here)
    all_scales = regrouped[1].reshape(layer_count, pages_here * head_count, 1, 2, heads_here)
    live_mask = send_live[None, :, :, None, None, None, None]
    slot_pages = jnp.where(live_mask, all_pages[:, physical], zero_page)
    slot_scales = jnp.where(live_mask, all_scales[:, physical], zero_scale)
    received = (
        lax.all_to_all(slot_pages, "rep", split_axis=1, concat_axis=1, tiled=True),
        lax.all_to_all(slot_scales, "rep", split_axis=1, concat_axis=1, tiled=True),
    )
    page_cache = received[0].reshape(layer_count, rep_count, capacity, span_max, 2, feat_here)
    scale_cache = received[1].reshape(layer_count, rep_count, capacity, pages_each, 2, heads_here)
    prompt_keys = page_cache[:, :, :, :, 0, :].reshape(
        layer_count, rep_count, capacity, span_max, heads_here, head_dim
    )
    prompt_values = page_cache[:, :, :, :, 1, :].reshape(
        layer_count, rep_count, capacity, span_max, heads_here, head_dim
    )
    query_rows = queries[0].reshape(
        layer_count, rep_count, capacity, steps_count, heads_here, head_dim
    )
    new_keys = new_kv[0][:, :, :, :, 0, :].reshape(
        layer_count, rep_count, capacity, steps_count, heads_here, head_dim
    )
    new_values = new_kv[0][:, :, :, :, 1, :].reshape(
        layer_count, rep_count, capacity, steps_count, heads_here, head_dim
    )
    score_root = math.sqrt(head_dim)
    key_scale = jnp.transpose(scale_cache[:, :, :, :, 0, :], (0, 1, 2, 4, 3))
    value_scale = jnp.transpose(scale_cache[:, :, :, :, 1, :], (0, 1, 2, 4, 3))
    prompt_dots = jnp.einsum(
        "lrcthd,lrckhd->lrchtk", query_rows, prompt_keys, preferred_element_type=jnp.float32
    )
    prompt_dots = prompt_dots.reshape(
        layer_count, rep_count, capacity, heads_here, steps_count, pages_each, page_rows
    )
    prompt_score = (
        prompt_dots * key_scale[:, :, :, :, None, :, None].astype(jnp.float32) / score_root
    )
    prompt_score = prompt_score.reshape(
        layer_count, rep_count, capacity, heads_here, steps_count, span_max
    )
    fresh_score = (
        jnp.einsum(
            "lrcthd,lrcuhd->lrchtu", query_rows, new_keys, preferred_element_type=jnp.float32
        )
        / score_root
    )
    visible = (jnp.arange(span_max, dtype=jnp.int32)[None, None, :] < slot_span[:, :, None])[
        None, :, :, None, None, :
    ]
    causal = (
        jnp.arange(steps_count, dtype=jnp.int32)[None, :]
        <= jnp.arange(steps_count, dtype=jnp.int32)[:, None]
    )
    row_max = jnp.maximum(
        jnp.max(jnp.where(visible, prompt_score, -jnp.inf), axis=-1, keepdims=True),
        jnp.max(jnp.where(causal, fresh_score, -jnp.inf), axis=-1, keepdims=True),
    )
    exp_prompt = jnp.where(visible, jnp.exp(prompt_score - row_max), 0.0)
    exp_fresh = jnp.where(causal, jnp.exp(fresh_score - row_max), 0.0)
    row_total = jnp.sum(exp_prompt, axis=-1, keepdims=True) + jnp.sum(
        exp_fresh, axis=-1, keepdims=True
    )
    value_weight = jnp.broadcast_to(
        value_scale[:, :, :, :, :, None], value_scale.shape + (page_rows,)
    )
    value_weight = value_weight.reshape(layer_count, rep_count, capacity, heads_here, span_max)[
        :, :, :, :, None, :
    ]
    prompt_weight = (exp_prompt * value_weight.astype(jnp.float32) / row_total).astype(jnp.bfloat16)
    fresh_weight = (exp_fresh / row_total).astype(jnp.bfloat16)
    attended = jnp.einsum(
        "lrchtk,lrckhd->lrcthd", prompt_weight, prompt_values, preferred_element_type=jnp.float32
    )
    attended = attended + jnp.einsum(
        "lrchtu,lrcuhd->lrcthd", fresh_weight, new_values, preferred_element_type=jnp.float32
    )
    attended = jnp.where(recv_live[None, :, :, None, None, None], attended, 0.0).astype(
        jnp.bfloat16
    )
    return (
        page_cache.reshape(1, layer_count, rep_count, capacity, span_max, 2, feat_here),
        scale_cache.reshape(1, layer_count, rep_count, capacity, pages_each, 2, heads_here),
        attended.reshape(1, layer_count, rep_count, capacity, steps_count, feat_here),
    )


def body(prompt_pages, page_scales, page_table, lengths, route, queries, new_kv):
    steps = plan(route, lengths)

    def direct(rounds, prompt_pages, page_scales, page_table, lengths, route, queries, new_kv):
        held = page_scales.shape[2]
        scales = page_scales.reshape(held, 2, 16, -1).transpose(2, 0, 1, 3)
        heads = scales.shape[3]
        scales = jnp.pad(jnp.tile(scales, (1, 1, 1, 4)), ((0, 0),) * 3 + ((0, 128 - 4 * heads),))
        own = jnp.arange(128) // heads == lax.axis_index("section")
        scales = jnp.where(own, scales, jnp.zeros((), scales.dtype))
        units = exchange(rounds, steps, page_table, prompt_pages, scales, queries, new_kv)
        return tuple(place(steps, units, queries))

    return lax.switch(
        steps[3, 0],
        [functools.partial(direct, rounds) for rounds in TIERS] + [padded],
        prompt_pages,
        page_scales,
        page_table,
        lengths,
        route,
        queries,
        new_kv,
    )


def solution(mesh):
    return jax.shard_map(
        body,
        mesh=mesh,
        in_specs=(
            P("rep", "section", "head", None, None, None),
            P("rep", "section", "head", None, None),
            P("rep", None),
            P(),
            P(),
            P("rep", None, None, None, None, ("section", "head")),
            P("rep", None, None, None, None, None, ("section", "head")),
        ),
        out_specs=(
            P("rep", None, None, None, None, None, ("section", "head")),
            P("rep", None, None, None, None, None, ("section", "head")),
            P("rep", None, None, None, None, ("section", "head")),
        ),
        check_vma=False,
    )
```

```python
import functools
import math

import jax
import jax.numpy as jnp
import numpy as np
from jax import lax
from jax.experimental import pallas as pl
from jax.experimental.pallas import tpu as pltpu
from jax.sharding import PartitionSpec as P

MESH = pl.DeviceIdType.MESH
NODES = 16
RING = NODES // 2
PORTS = 3
TIERS = (13, 14, 16)
ROUNDS = TIERS[-1]
PARTS = 4
REQS = 8
PAGE = 16
OFFSETS = (0, 0, 0, 0)

ROUTES = (
    0o5555555222222210, 0o5555555222222201, 0o4645121222121045, 0o5555212221210154,
    0o4612132222104545, 0o5531222222015554, 0o2212122210555646, 0o3121222101545455,
    0o1313121055555512, 0o2222210155555451, 0o1312105545565515, 0o2222015455555521,
    0o1310554545561212, 0o2201555555542221, 0o1055555555121212, 0o0155555454222222,
    0o5555552522222210, 0o5555552522222201, 0o5546222322221045, 0o5555522122220154,
    0o4526221222105645, 0o2122312131015554, 0o4323221310464555, 0o2232312101646565,
    0o2222231045454555, 0o3122220155646521, 0o2222105556454623, 0o3131015555542231,
    0o2210455656452312, 0o2101555564555232, 0o1045455546131312, 0o0154546565312122,
)


def links_of(source, dest, code):
    if code == 0:
        return []
    z, y = divmod(source, 2)
    step, mode = (1, (code - 1) % 3) if code <= 3 else (-1, (code - 1) % 3)
    cross = y != dest % 2
    hops = [2] if (cross and mode == 0) or (not cross and mode == 2) else []
    hops += [0 if step > 0 else 1] * (((dest // 2 - z) * step) % RING)
    if (cross and mode != 0) or (not cross and mode == 2):
        hops += [2]
    links = []
    for port in hops:
        links.append((z * 2 + y) * PORTS + port)
        if port == 2:
            y = 1 - y
        else:
            z = (z + (1 if port == 0 else -1)) % RING
    assert z * 2 + y == dest and len(links) < 8
    return links


def path_table():
    table = np.zeros((2, NODES, 8, NODES), np.float32)
    for rank in range(2):
        for source in range(NODES):
            for dest in range(NODES):
                code = (ROUTES[rank * NODES + source] >> (3 * dest)) & 7
                for hop, link in enumerate(links_of(source, dest, code)):
                    table[rank, dest, hop, source] = link + 1
    return table.reshape(2 * NODES * 8, NODES)


def plan_kernel(table_ref, inputs_ref, out_ref, sends, slots, spans):
    f32 = jnp.float32
    lane = lax.broadcasted_iota(jnp.int32, (1, 128), 1)
    source = lane // REQS
    order = lane % REQS
    pick = lax.broadcasted_iota(jnp.int32, (REQS, 128), 1) % REQS
    pick = pick == lax.broadcasted_iota(jnp.int32, (REQS, 128), 0)
    pick = jnp.where(pick, 1.0, 0.0).astype(jnp.bfloat16)

    def flat(ref):
        x = jnp.dot(ref.astype(jnp.bfloat16), pick, preferred_element_type=f32)
        x = jnp.where(node == source, x, 0.0)
        return jnp.sum(x, axis=0, keepdims=True)

    node = lax.broadcasted_iota(jnp.int32, (NODES, 128), 0)
    route = flat(inputs_ref[:NODES]).astype(jnp.int32)
    length = flat(inputs_ref[NODES:])
    rank = jnp.zeros_like(route)
    for back in range(1, REQS):
        earlier = pltpu.roll(route, back, axis=1)
        rank = rank + jnp.where((earlier == route) & (order >= back), 1, 0)
    count = jnp.sum(jnp.where(node == route, 1.0, 0.0), axis=1, keepdims=True)
    most = jnp.max(count, axis=0, keepdims=True)
    nodes = lax.broadcasted_iota(jnp.int32, (NODES, 1), 0).astype(f32)
    hot = jnp.min(jnp.where(count == most, nodes, 99.0), axis=0, keepdims=True).astype(jnp.int32)
    hot_z, hot_y = hot // 2, hot % 2

    def relative(x):
        y = x % 2
        return ((x // 2 - hot_z + RING) % RING) * 2 + (y + hot_y - 2 * y * hot_y)

    source_rel, dest_rel = relative(source), relative(route)
    from_one = jnp.where(node == source_rel, 1.0, 0.0).astype(jnp.bfloat16)
    every = jnp.dot(table_ref[...], from_one, preferred_element_type=f32)
    row = lax.broadcasted_iota(jnp.int32, (2 * NODES * 8, 128), 0) // 8
    every = jnp.where(row == rank * NODES + dest_rel, every, 0.0)
    path = every[0:8]
    for i in range(1, 2 * NODES):
        path = path + every[8 * i : 8 * i + 8]
    me = relative(jnp.zeros((1, 1), jnp.int32) + lax.axis_index("rep"))
    me_z, me_y = me // 2, me % 2
    up, down = (me_z + 1) % RING, (me_z + RING - 1) % RING
    to_me = (down * 2 + me_y, up * 2 + me_y, me_z * 2 + 1 - me_y)
    out_link = [(me * PORTS + k + 1).astype(f32) for k in range(PORTS)]
    in_link = [(to_me[k] * PORTS + k + 1).astype(f32) for k in range(PORTS)]
    link = lax.broadcasted_iota(jnp.int32, (NODES * PORTS, 128), 0).astype(f32) + 1.0
    tie = (127 - lane).astype(f32)
    hop_row = lax.broadcasted_iota(jnp.int32, (8, 128), 0)
    held = jnp.where(source_rel == me, order, 0).astype(f32)
    home = dest_rel == me
    own_slot = jnp.where(home, source * 2 + rank, 0).astype(f32)
    own_span = jnp.where(home, length, 0.0)
    for ref in (sends, slots, spans):
        ref[...] = jnp.zeros_like(ref)
    fine = []
    for t in range(ROUNDS):
        now = path[0:1]
        if t in TIERS:
            fine.append(jnp.max(now, axis=1, keepdims=True) == 0.0)
        left = jnp.sum(jnp.where(path > 0.0, 1.0, 0.0), axis=0, keepdims=True)
        key = left * 128.0 + tie
        asks = link == now
        first = jnp.max(jnp.where(asks, key, -1.0), axis=1, keepdims=True)
        wins = jnp.where(asks & (first == key), 1.0, 0.0)
        moves = jnp.max(wins, axis=0, keepdims=True) > 0.0
        for k in range(PORTS):
            leaves = moves & (now == out_link[k])
            sends[PORTS * t + k : PORTS * t + k + 1] = jnp.where(leaves, held, 0.0)
        for k in range(PORTS):
            comes = moves & (now == in_link[k])
            held = jnp.where(comes, float(REQS + PORTS * t + k), held)
            slots[PORTS * t + k : PORTS * t + k + 1] = jnp.where(comes, own_slot, 0.0)
            spans[PORTS * t + k : PORTS * t + k + 1] = jnp.where(comes, own_span, 0.0)
        later = jnp.where(hop_row < 7, pltpu.roll(path, 7, axis=0), 0.0)
        path = jnp.where(moves, later, path)
    fine.append(jnp.max(path[0:1], axis=1, keepdims=True) == 0.0)
    tier = sum(jnp.where(done, 0.0, 1.0) for done in fine)
    square = lax.broadcasted_iota(jnp.int32, (128, 128), 0) == lax.broadcasted_iota(
        jnp.int32, (128, 128), 1
    )

    def lay(rows):
        sums = jnp.sum(rows, axis=1, keepdims=True)
        n = rows.shape[0]
        return jnp.sum(jnp.where(square[:n], sums, 0.0), axis=0, keepdims=True)

    slot = lax.broadcasted_iota(jnp.int32, (2 * NODES, 128), 0)
    mine = (slot == source * 2 + rank) & home
    out = [
        lay(sends[...]),
        lay(jnp.where(mine, held, 0.0)),
        lay(jnp.where(mine, length, 0.0)),
        jnp.where(lane >= 0, tier, 0.0),
        lay(slots[...]),
        lay(spans[...]),
        jnp.zeros((2, 128), f32),
    ]
    out_ref[...] = jnp.concatenate(out, axis=0).astype(jnp.int32)


def plan(route, lengths):
    return pl.pallas_call(
        plan_kernel,
        out_shape=jax.ShapeDtypeStruct((8, 128), jnp.int32),
        in_specs=[pl.BlockSpec(memory_space=pltpu.VMEM)] * 2,
        out_specs=pl.BlockSpec(memory_space=pltpu.VMEM),
        scratch_shapes=[pltpu.VMEM((128, 128), jnp.float32)] * 3,
    )(jnp.asarray(path_table(), jnp.bfloat16), jnp.concatenate([route, lengths], axis=0))


def attend(known, new, queries, scale, span):
    f32 = jnp.float32
    bf16 = jnp.bfloat16
    layers = len(known)
    steps, feats = queries[0].shape
    heads = feats // 128
    rows = known[0].shape[0]
    total_rows = rows + new[0].shape[0]
    per_layer = heads * steps
    over = (((1,), (1,)), ((), ()))
    row = lax.broadcasted_iota(jnp.int32, (total_rows, 128), 0)
    lane = lax.broadcasted_iota(jnp.int32, (total_rows, 128), 1)
    even = row % 2 == 0
    part = rows // PARTS
    page = row % part // (part // 2)
    token = PAGE * page + row // part * (PAGE // PARTS) + row % (part // 2) // 2
    fresh = (row >= rows) & ((row - rows) // 2 <= lane % steps)
    valid = even & (((row < rows) & (token < span)) | fresh)
    own_head = lax.broadcasted_iota(jnp.int32, (128, 128), 0)
    own_head = own_head == lax.broadcasted_iota(jnp.int32, (128, 128), 1) // steps
    own_head = jnp.where(own_head, 1.0, 0.0).astype(bf16)
    block = lax.broadcasted_iota(jnp.int32, (per_layer, feats), 1) // 128
    block = block == lax.broadcasted_iota(jnp.int32, (per_layer, feats), 0) // steps

    both = [jnp.concatenate([known[l], new[l]], axis=0) for l in range(layers)]
    query = []
    for one in queries:
        one = jnp.concatenate([one.astype(f32)] * heads, axis=0)
        query.append(jnp.where(block, one, 0.0))
    query.append(jnp.zeros((128 - layers * per_layer, feats), f32))
    query = jnp.concatenate(query, axis=0).astype(bf16)
    score = lax.dot_general(both[0], query, over, preferred_element_type=f32)
    for l in range(1, layers):
        other = lax.dot_general(both[l], query, over, preferred_element_type=f32)
        score = jnp.where(lane // per_layer == l, other, score)
    scale = scale.astype(f32)
    scale = ((scale[0] + scale[1]) + (scale[2] + scale[3])).reshape(4, 128)
    scale = jnp.concatenate([scale, jnp.zeros((12, 128), f32)], axis=0).astype(bf16)
    scale = jnp.dot(scale, own_head, preferred_element_type=f32)
    factor = jnp.where(
        page == 0,
        jnp.where(even, scale[0:1], scale[1:2]),
        jnp.where(even, scale[2:3], scale[3:4]),
    )
    factor = jnp.where(row < rows, factor, 1.0)
    score = jnp.where(valid, score * factor / math.sqrt(128), -jnp.inf)
    power = jnp.exp(score - jnp.max(score, axis=0, keepdims=True))
    total = jnp.sum(power, axis=0, keepdims=True)
    weight = (pltpu.roll(power, 1, axis=0) * factor / total).T
    results = []
    for l in range(layers):
        own = weight[per_layer * l : per_layer * (l + 1)].astype(bf16)
        result = jnp.dot(own, both[l], preferred_element_type=f32)
        parts = [
            result[steps * h : steps * h + steps, 128 * h : 128 * h + 128] for h in range(heads)
        ]
        results.append(jnp.concatenate(parts, axis=1).astype(bf16))
    return results


def exchange_kernel(rounds, plan_ref, table_ref, pages, scales, query_hbm, new_hbm, *refs):
    streams = PARTS + 1
    stores = refs[:streams]
    att = refs[streams]
    refs = refs[streams + 1 :]
    groups = refs[:streams]
    lands = refs[streams : 2 * streams]
    packs = refs[2 * streams : 3 * streams]
    queries, news, group_send, group_recv, send_sem, recv_sem, new_sem = refs[3 * streams :]
    rep = lax.axis_index("rep")
    section = lax.axis_index("section")
    head = lax.axis_index("head")
    tokens = groups[0].shape[2]
    held = pages.shape[2]
    feats = groups[0].shape[4]
    layers, _, steps, _ = queries.shape

    peers = []
    for o in range(16):
        peers.append((lax.rem(section + o // 4, 4), lax.rem(head + o % 4, 4)))
    neighbours = (
        lax.rem(rep + 2, NODES),
        lax.rem(rep + NODES - 2, NODES),
        rep + 1 - 2 * lax.rem(rep, 2),
    )
    barrier = pltpu.get_barrier_semaphore()
    for s, h in peers[1:]:
        pl.semaphore_signal(barrier, inc=1, device_id=(rep, s, h), device_id_type=MESH)
    for n in neighbours:
        pl.semaphore_signal(barrier, inc=1, device_id=(n, section, head), device_id_type=MESH)
    pl.semaphore_wait(barrier, 15 + PORTS)

    def block(i, group):
        if i == PARTS:
            return scales.at[group]
        columns = pl.ds(pl.multiple_of(group * feats, 128), feats)
        return pages.at[0, 0, :, pl.ds(tokens * i, tokens), :, columns]

    def place(i, s, h):
        return groups[i].at[s, pl.ds(held * h, held)]

    def regroup(i, o):
        s, h = peers[o]
        return pltpu.make_async_remote_copy(
            src_ref=block(i, s * 4 + h),
            dst_ref=place(i, section, head),
            send_sem=group_send.at[i, o],
            recv_sem=group_recv.at[i, o],
            device_id=(rep, s, h),
            device_id_type=MESH,
        )

    def regroup_own(i):
        return pltpu.make_async_copy(
            block(i, section * 4 + head), place(i, section, head), group_recv.at[i, 0]
        )

    order = [PARTS] + list(range(PARTS))
    for i in order:
        for o in range(1, 16):
            regroup(i, o).start()
        regroup_own(i).start()
    load_query = pltpu.make_async_copy(query_hbm, queries, new_sem.at[0])
    load_new = pltpu.make_async_copy(new_hbm, news, new_sem.at[1])
    load_query.start()
    load_new.start()

    def send(i, slot, k):
        return pltpu.make_async_remote_copy(
            src_ref=packs[i].at[slot, k],
            dst_ref=lands[i].at[slot, k],
            send_sem=send_sem.at[i, slot, k],
            recv_sem=recv_sem.at[i, slot, k],
            device_id=(neighbours[k], section, head),
            device_id_type=MESH,
        )

    def compose(i, t, slot):
        for k in range(PORTS):
            packs[i][slot, k] = stores[i][plan_ref[0, PORTS * t + k]]
        for k in range(PORTS):
            send(i, slot, k).start()

    def arrive(i, t, slot):
        for k in range(PORTS):
            send(i, slot, k).wait_recv()
        for k in range(PORTS):
            stores[i][REQS + PORTS * t + k] = lands[i][slot, k]

    def attend_unit(at, unit, slot, span):
        known = [
            jnp.concatenate(
                [stores[i][unit, l].reshape(4 * tokens, feats) for i in range(PARTS)], axis=0
            )
            for l in range(layers)
        ]
        new = [news[l, slot].reshape(2 * steps, feats) for l in range(layers)]
        query = [queries[l, slot] for l in range(layers)]
        results = attend(known, new, query, stores[PARTS][unit], span)
        for l in range(layers):
            att[at, l] = results[l]

    def attend_own():
        for c in range(2):
            slot = 2 * rep + c
            attend_unit(c, plan_ref[1, slot], slot, plan_ref[2, slot])

    def attend_arrived(t):
        for k in range(PORTS):
            at = PORTS * t + k
            attend_unit(REQS + at, REQS + at, plan_ref[4, at], plan_ref[5, at])

    lag = OFFSETS + (0,)
    most = max(lag)

    def first(i):
        regroup_own(i).wait()
        for o in range(1, 16):
            regroup(i, o).wait_recv()
        for q in range(REQS):
            for j in range(2):
                stores[i][q, :, j] = groups[i][:, table_ref[0, 2 * q + j]]
        compose(i, 0, 0)

    def attend_at(time, k):
        if isinstance(time, int) and not 0 < time - most <= rounds:
            return
        at = PORTS * (time - most - 1) + k
        attend_unit(REQS + at, REQS + at, plan_ref[4, at], plan_ref[5, at])

    def beat(time):
        for n, i in enumerate(order):
            t = time - lag[i]
            if not isinstance(time, int):
                slot = lax.rem(t, 2)
                arrive(i, t - 1, 1 - slot)
                for k in range(PORTS):
                    send(i, slot, k).wait_send()
                compose(i, t, slot)
            elif t == 0:
                first(i)
            elif 0 < t <= rounds:
                arrive(i, t - 1, (t - 1) % 2)
                if t >= 2 and t < rounds:
                    for k in range(PORTS):
                        send(i, t % 2, k).wait_send()
                if t < rounds:
                    compose(i, t, t % 2)
            if n == PARTS:
                for k in range(PORTS):
                    attend_at(time, k)

    for time in range(most + 2):
        beat(time)
        if time == most:
            load_query.wait()
            load_new.wait()
            attend_own()

    def one(time, carry):
        beat(time)
        return carry

    lax.fori_loop(most + 2, rounds, one, 0)
    for time in range(rounds, rounds + most + 2):
        beat(time)
    for i in order:
        for slot in range(2):
            for k in range(PORTS):
                send(i, slot, k).wait_send()
        for o in range(1, 16):
            regroup(i, o).wait_send()


def exchange(rounds, steps, page_table, pages, scales, queries, new_kv):
    layers, nodes, cap, step_count, feats = queries.shape[1:]
    held = pages.shape[2]
    tokens = pages.shape[3] // PARTS
    store = REQS + PORTS * rounds
    units = [(tokens, 2, feats)] * PARTS + [(2, 128)]
    bf16 = jnp.bfloat16
    anywhere = pl.BlockSpec(memory_space=pl.ANY)
    smem = pl.BlockSpec(memory_space=pltpu.SMEM)
    vmem = pl.BlockSpec(memory_space=pltpu.VMEM)
    scratch = [pltpu.VMEM((layers, 4 * held) + u, bf16) for u in units]
    scratch += [pltpu.VMEM((2, PORTS, layers, 2) + u, bf16) for u in units] * 2
    query_shape = (layers, nodes * cap, step_count, feats)
    new_shape = (layers, nodes * cap, step_count, 2, feats)
    scratch += [pltpu.VMEM(query_shape, bf16), pltpu.VMEM(new_shape, bf16)]
    dma = pltpu.SemaphoreType.DMA
    streams = PARTS + 1
    scratch += [dma((streams, 16)), dma((streams, 16))]
    scratch += [dma((streams, 2, PORTS)), dma((streams, 2, PORTS)), dma((2,))]
    return pl.pallas_call(
        functools.partial(exchange_kernel, rounds),
        out_shape=[jax.ShapeDtypeStruct((store, layers, 2) + u, bf16) for u in units]
        + [jax.ShapeDtypeStruct((store, layers, step_count, feats), bf16)],
        in_specs=[smem, smem] + [anywhere] * 4,
        out_specs=[vmem] * (streams + 1),
        scratch_shapes=scratch,
        compiler_params=pltpu.CompilerParams(
            collective_id=rounds, has_side_effects=True, vmem_limit_bytes=40 << 20
        ),
        cost_estimate=pl.CostEstimate(flops=0, bytes_accessed=20 << 20, transcendentals=0),
    )(
        steps,
        page_table,
        pages,
        scales,
        queries.reshape(query_shape),
        new_kv.reshape(new_shape),
    )


def place_kernel(plan_ref, *refs):
    units, scales, att = refs[:PARTS], refs[PARTS], refs[PARTS + 1]
    cache_hbm, scales_ref, att_hbm, zero_unit, zero_att, sems = refs[PARTS + 2 :]
    layers, slots, _, _, heads = scales_ref.shape
    tokens = units[0].shape[3]
    cap = 2
    rep = lax.axis_index("rep")
    zero_unit[...] = jnp.zeros_like(zero_unit)
    zero_att[...] = jnp.zeros_like(zero_att)

    def copies(i, live):
        unit = plan_ref[1, i]
        at = jnp.where(i // cap == rep, i % cap, unit)
        out = []
        for s in range(PARTS):
            to = cache_hbm.at[0, :, i // cap, i % cap, :, pl.ds(tokens * s, tokens)]
            source = units[s].at[unit] if live else zero_unit
            out.append(pltpu.make_async_copy(source, to, sems.at[i, s]))
        source = att.at[at] if live else zero_att
        to = att_hbm.at[0, :, i // cap, i % cap]
        return out + [pltpu.make_async_copy(source, to, sems.at[i, PARTS])]

    @pl.loop(0, slots)
    def _(i):
        @pl.when(plan_ref[2, i] > 0)
        def _():
            for copy in copies(i, True):
                copy.start()
            scale = scales[plan_ref[1, i]]
            for l in range(layers):
                scales_ref[l, i] = scale[l][:, :, heads * l : heads * l + heads]

        @pl.when(plan_ref[2, i] == 0)
        def _():
            for copy in copies(i, False):
                copy.start()
            for l in range(layers):
                scales_ref[l, i] = jnp.zeros((2, 2, heads), scales_ref.dtype)

    @pl.loop(0, slots)
    def _(i):
        for copy in copies(i, False):
            copy.wait()


def place(steps, units, queries):
    layers, nodes, cap, step_count, feats = queries.shape[1:]
    heads = feats // 128
    bf16 = jnp.bfloat16
    anywhere = pl.BlockSpec(memory_space=pl.ANY)
    vmem = pl.BlockSpec(memory_space=pltpu.VMEM)
    smem = pl.BlockSpec(memory_space=pltpu.SMEM)
    cache, scales, attention = pl.pallas_call(
        place_kernel,
        in_specs=[smem] + [vmem] * len(units),
        out_specs=[anywhere, vmem, anywhere],
        out_shape=[
            jax.ShapeDtypeStruct((1, layers, nodes, cap, 2, PAGE, 2, feats), bf16),
            jax.ShapeDtypeStruct((layers, nodes * cap, 2, 2, heads), bf16),
            jax.ShapeDtypeStruct(queries.shape, bf16),
        ],
        scratch_shapes=[
            pltpu.VMEM(units[0].shape[1:], bf16),
            pltpu.VMEM(units[PARTS + 1].shape[1:], bf16),
            pltpu.SemaphoreType.DMA((nodes * cap, PARTS + 1)),
        ],
        compiler_params=pltpu.CompilerParams(vmem_limit_bytes=40 << 20),
    )(steps, *units)
    cache = cache.reshape(1, layers, nodes, cap, 2 * PAGE, 2, feats)
    return cache, scales.reshape(1, layers, nodes, cap, 2, 2, heads), attention


def slot_ranks(route):
    req_ids = jnp.arange(route.shape[1], dtype=jnp.int32)
    same_dest = route[:, :, None] == route[:, None, :]
    earlier = req_ids[None, :] < req_ids[:, None]
    return jnp.sum((same_dest & earlier[None]).astype(jnp.int32), axis=2)


def padded(prompt_pages, page_scales, page_table, lengths, route, queries, new_kv):
    rep_count = lax.axis_size("rep")
    section_count = lax.axis_size("section")
    head_count = lax.axis_size("head")
    replica = lax.axis_index("rep")
    layers_here = prompt_pages.shape[1]
    pages_here = prompt_pages.shape[2]
    page_rows = prompt_pages.shape[3]
    feature_count = prompt_pages.shape[5]
    heads_total = page_scales.shape[4]
    head_dim = feature_count // heads_total
    group_count = section_count * head_count
    feat_here = feature_count // group_count
    heads_here = heads_total // group_count
    req_count = route.shape[1]
    capacity = max(2, req_count // rep_count)
    pages_each = page_table.shape[1] // req_count
    layer_count = layers_here * section_count
    span_max = page_rows * pages_each
    steps_count = queries.shape[4]
    req_ids = jnp.arange(req_count, dtype=jnp.int32)
    dest_ids = jnp.arange(rep_count, dtype=jnp.int32)
    cap_ids = jnp.arange(capacity, dtype=jnp.int32)
    page_ids = jnp.arange(pages_each, dtype=jnp.int32)
    slot_rank = slot_ranks(route)
    own_route = lax.dynamic_index_in_dim(route, replica, 0, keepdims=False)
    own_rank = lax.dynamic_index_in_dim(slot_rank, replica, 0, keepdims=False)
    send_match = (own_route[None, None, :] == dest_ids[:, None, None]) & (
        own_rank[None, None, :] == cap_ids[None, :, None]
    )
    send_live = jnp.any(send_match, axis=2)
    send_request = jnp.sum(jnp.where(send_match, req_ids[None, None, :], 0), axis=2)
    physical = page_table[0][send_request[:, :, None] * pages_each + page_ids[None, None, :]]
    recv_match = (route[:, None, :] == replica) & (slot_rank[:, None, :] == cap_ids[None, :, None])
    recv_live = jnp.any(recv_match, axis=2)
    slot_span = jnp.sum(jnp.where(recv_match, lengths[:, None, :], 0), axis=2)
    page_view = prompt_pages[0].reshape(
        layers_here, pages_here, page_rows, 2, section_count, head_count, feat_here
    )
    scale_view = page_scales[0].reshape(
        layers_here, pages_here, 1, 2, section_count, head_count, heads_here
    )
    zero_page = jnp.zeros((), prompt_pages.dtype)
    zero_scale = jnp.zeros((), page_scales.dtype)
    regrouped = (
        lax.all_to_all(
            lax.all_to_all(page_view, "section", split_axis=4, concat_axis=0, tiled=True),
            "head",
            split_axis=5,
            concat_axis=1,
            tiled=True,
        ),
        lax.all_to_all(
            lax.all_to_all(scale_view, "section", split_axis=4, concat_axis=0, tiled=True),
            "head",
            split_axis=5,
            concat_axis=1,
            tiled=True,
        ),
    )
    all_pages = regrouped[0].reshape(layer_count, pages_here * head_count, page_rows, 2, feat_here)
    all_scales = regrouped[1].reshape(layer_count, pages_here * head_count, 1, 2, heads_here)
    live_mask = send_live[None, :, :, None, None, None, None]
    slot_pages = jnp.where(live_mask, all_pages[:, physical], zero_page)
    slot_scales = jnp.where(live_mask, all_scales[:, physical], zero_scale)
    received = (
        lax.all_to_all(slot_pages, "rep", split_axis=1, concat_axis=1, tiled=True),
        lax.all_to_all(slot_scales, "rep", split_axis=1, concat_axis=1, tiled=True),
    )
    page_cache = received[0].reshape(layer_count, rep_count, capacity, span_max, 2, feat_here)
    scale_cache = received[1].reshape(layer_count, rep_count, capacity, pages_each, 2, heads_here)
    prompt_keys = page_cache[:, :, :, :, 0, :].reshape(
        layer_count, rep_count, capacity, span_max, heads_here, head_dim
    )
    prompt_values = page_cache[:, :, :, :, 1, :].reshape(
        layer_count, rep_count, capacity, span_max, heads_here, head_dim
    )
    query_rows = queries[0].reshape(
        layer_count, rep_count, capacity, steps_count, heads_here, head_dim
    )
    new_keys = new_kv[0][:, :, :, :, 0, :].reshape(
        layer_count, rep_count, capacity, steps_count, heads_here, head_dim
    )
    new_values = new_kv[0][:, :, :, :, 1, :].reshape(
        layer_count, rep_count, capacity, steps_count, heads_here, head_dim
    )
    score_root = math.sqrt(head_dim)
    key_scale = jnp.transpose(scale_cache[:, :, :, :, 0, :], (0, 1, 2, 4, 3))
    value_scale = jnp.transpose(scale_cache[:, :, :, :, 1, :], (0, 1, 2, 4, 3))
    prompt_dots = jnp.einsum(
        "lrcthd,lrckhd->lrchtk", query_rows, prompt_keys, preferred_element_type=jnp.float32
    )
    prompt_dots = prompt_dots.reshape(
        layer_count, rep_count, capacity, heads_here, steps_count, pages_each, page_rows
    )
    prompt_score = (
        prompt_dots * key_scale[:, :, :, :, None, :, None].astype(jnp.float32) / score_root
    )
    prompt_score = prompt_score.reshape(
        layer_count, rep_count, capacity, heads_here, steps_count, span_max
    )
    fresh_score = (
        jnp.einsum(
            "lrcthd,lrcuhd->lrchtu", query_rows, new_keys, preferred_element_type=jnp.float32
        )
        / score_root
    )
    visible = (jnp.arange(span_max, dtype=jnp.int32)[None, None, :] < slot_span[:, :, None])[
        None, :, :, None, None, :
    ]
    causal = (
        jnp.arange(steps_count, dtype=jnp.int32)[None, :]
        <= jnp.arange(steps_count, dtype=jnp.int32)[:, None]
    )
    row_max = jnp.maximum(
        jnp.max(jnp.where(visible, prompt_score, -jnp.inf), axis=-1, keepdims=True),
        jnp.max(jnp.where(causal, fresh_score, -jnp.inf), axis=-1, keepdims=True),
    )
    exp_prompt = jnp.where(visible, jnp.exp(prompt_score - row_max), 0.0)
    exp_fresh = jnp.where(causal, jnp.exp(fresh_score - row_max), 0.0)
    row_total = jnp.sum(exp_prompt, axis=-1, keepdims=True) + jnp.sum(
        exp_fresh, axis=-1, keepdims=True
    )
    value_weight = jnp.broadcast_to(
        value_scale[:, :, :, :, :, None], value_scale.shape + (page_rows,)
    )
    value_weight = value_weight.reshape(layer_count, rep_count, capacity, heads_here, span_max)[
        :, :, :, :, None, :
    ]
    prompt_weight = (exp_prompt * value_weight.astype(jnp.float32) / row_total).astype(jnp.bfloat16)
    fresh_weight = (exp_fresh / row_total).astype(jnp.bfloat16)
    attended = jnp.einsum(
        "lrchtk,lrckhd->lrcthd", prompt_weight, prompt_values, preferred_element_type=jnp.float32
    )
    attended = attended + jnp.einsum(
        "lrchtu,lrcuhd->lrcthd", fresh_weight, new_values, preferred_element_type=jnp.float32
    )
    attended = jnp.where(recv_live[None, :, :, None, None, None], attended, 0.0).astype(
        jnp.bfloat16
    )
    return (
        page_cache.reshape(1, layer_count, rep_count, capacity, span_max, 2, feat_here),
        scale_cache.reshape(1, layer_count, rep_count, capacity, pages_each, 2, heads_here),
        attended.reshape(1, layer_count, rep_count, capacity, steps_count, feat_here),
    )


def body(prompt_pages, page_scales, page_table, lengths, route, queries, new_kv):
    steps = plan(route, lengths)

    def direct(rounds, prompt_pages, page_scales, page_table, lengths, route, queries, new_kv):
        held = page_scales.shape[2]
        scales = page_scales.reshape(held, 2, 16, -1).transpose(2, 0, 1, 3)
        heads = scales.shape[3]
        scales = jnp.pad(jnp.tile(scales, (1, 1, 1, 4)), ((0, 0),) * 3 + ((0, 128 - 4 * heads),))
        own = jnp.arange(128) // heads == lax.axis_index("section")
        scales = jnp.where(own, scales, jnp.zeros((), scales.dtype))
        units = exchange(rounds, steps, page_table, prompt_pages, scales, queries, new_kv)
        return tuple(place(steps, units, queries))

    return lax.switch(
        len(TIERS) - steps[3, 0],
        [padded] + [functools.partial(direct, rounds) for rounds in TIERS[::-1]],
        prompt_pages,
        page_scales,
        page_table,
        lengths,
        route,
        queries,
        new_kv,
    )


def solution(mesh):
    return jax.shard_map(
        body,
        mesh=mesh,
        in_specs=(
            P("rep", "section", "head", None, None, None),
            P("rep", "section", "head", None, None),
            P("rep", None),
            P(),
            P(),
            P("rep", None, None, None, None, ("section", "head")),
            P("rep", None, None, None, None, None, ("section", "head")),
        ),
        out_specs=(
            P("rep", None, None, None, None, None, ("section", "head")),
            P("rep", None, None, None, None, None, ("section", "head")),
            P("rep", None, None, None, None, ("section", "head")),
        ),
        check_vma=False,
    )
```

```python
import functools
import math

import jax
import jax.numpy as jnp
import numpy as np
from jax import lax
from jax.experimental import pallas as pl
from jax.experimental.pallas import tpu as pltpu
from jax.sharding import PartitionSpec as P

MESH = pl.DeviceIdType.MESH
NODES = 16
RING = NODES // 2
PORTS = 3
TIERS = (12, 13, 16)
ROUNDS = TIERS[-1]
PARTS = 4
REQS = 8
PAGE = 16
OFFSETS = (0, 0, 0, 0)

ROUTES = (
    0o5555555222222210, 0o5555555222222201, 0o4642121222221045, 0o5555212221210154,
    0o4612132222104545, 0o5531222222015554, 0o2212122210555646, 0o3121222101655455,
    0o1313221055555512, 0o2222220155555451, 0o1312105546565515, 0o2222015455555521,
    0o1310554545561212, 0o2201555555542221, 0o1055555555151212, 0o0155555454222222,
    0o5555461213122210, 0o5565652131222201, 0o5646262313221045, 0o5464522132320164,
    0o2523221322105645, 0o2152312131015454, 0o1323231310464515, 0o2232313201546565,
    0o2222131046565645, 0o3121210154656521, 0o2213104555454323, 0o2132015565655431,
    0o2210465656454322, 0o3101646564653432, 0o1056565556422322, 0o0165646522223232,
    0o5555555523222210, 0o5555553522222201, 0o4642122222221045, 0o5555322221220154,
    0o4612122222104545, 0o5521222222015554, 0o1212222210554546, 0o2222222201545455,
    0o1223121045555642, 0o2222320155546451, 0o1312105655455512, 0o2222015565555521,
    0o1310454555551212, 0o2201545555552221, 0o1055555555121313, 0o0155555455222222,
    0o5555461312222210, 0o6555655222322201, 0o4526221212221045, 0o6421213222220164,
    0o1223222213105655, 0o2432212132016564, 0o4323231210465622, 0o3531312101656524,
    0o2312231056464655, 0o3231210155655525, 0o1223104646561325, 0o3132015555656431,
    0o1210555646465522, 0o2101655465242532, 0o1056455646252222, 0o0154556522552232,
)
TABLES = 4


def links_of(source, dest, code):
    if code == 0:
        return []
    z, y = divmod(source, 2)
    step, mode = (1, (code - 1) % 3) if code <= 3 else (-1, (code - 1) % 3)
    cross = y != dest % 2
    hops = [2] if (cross and mode == 0) or (not cross and mode == 2) else []
    hops += [0 if step > 0 else 1] * (((dest // 2 - z) * step) % RING)
    if (cross and mode != 0) or (not cross and mode == 2):
        hops += [2]
    links = []
    for port in hops:
        links.append((z * 2 + y) * PORTS + port)
        if port == 2:
            y = 1 - y
        else:
            z = (z + (1 if port == 0 else -1)) % RING
    assert z * 2 + y == dest and len(links) < 8
    return links


def path_table():
    table = np.zeros((TABLES, 2, NODES, 8, NODES), np.float32)
    for n, rank in np.ndindex(TABLES, 2):
        for source, dest in np.ndindex(NODES, NODES):
            row, digit = source, dest
            if n % 2:
                row, digit = ((RING - x // 2) % RING * 2 + x % 2 for x in (source, dest))
            code = (ROUTES[n // 2 * 32 + rank * NODES + row] >> (3 * digit)) & 7
            if n % 2 and code:
                code = (code + 2) % 6 + 1
            for hop, link in enumerate(links_of(source, dest, code)):
                table[n, rank, dest, hop, source] = link + 1
    return table.reshape(TABLES * 2 * NODES * 8, NODES)


def plan_kernel(table_ref, inputs_ref, out_ref, sends, slots, spans):
    f32 = jnp.float32
    lane = lax.broadcasted_iota(jnp.int32, (1, 128), 1)
    source = lane // REQS
    order = lane % REQS
    pick = lax.broadcasted_iota(jnp.int32, (REQS, 128), 1) % REQS
    pick = pick == lax.broadcasted_iota(jnp.int32, (REQS, 128), 0)
    pick = jnp.where(pick, 1.0, 0.0).astype(jnp.bfloat16)

    def flat(ref):
        x = jnp.dot(ref.astype(jnp.bfloat16), pick, preferred_element_type=f32)
        x = jnp.where(node == source, x, 0.0)
        return jnp.sum(x, axis=0, keepdims=True)

    node = lax.broadcasted_iota(jnp.int32, (NODES, 128), 0)
    route = flat(inputs_ref[:NODES]).astype(jnp.int32)
    length = flat(inputs_ref[NODES:])
    rank = jnp.zeros_like(route)
    for back in range(1, REQS):
        earlier = pltpu.roll(route, back, axis=1)
        rank = rank + jnp.where((earlier == route) & (order >= back), 1, 0)
    count = jnp.sum(jnp.where(node == route, 1.0, 0.0), axis=1, keepdims=True)
    most = jnp.max(count, axis=0, keepdims=True)
    nodes = lax.broadcasted_iota(jnp.int32, (NODES, 1), 0).astype(f32)
    hot = jnp.min(jnp.where(count == most, nodes, 99.0), axis=0, keepdims=True).astype(jnp.int32)
    hot_z, hot_y = hot // 2, hot % 2

    def relative(x):
        y = x % 2
        return ((x // 2 - hot_z + RING) % RING) * 2 + (y + hot_y - 2 * y * hot_y)

    source_rel, dest_rel = relative(source), relative(route)
    from_one = jnp.where(node == source_rel, 1.0, 0.0).astype(jnp.bfloat16)
    link = lax.broadcasted_iota(jnp.int32, (NODES * PORTS, 128), 0).astype(f32) + 1.0
    length_of_table = 2 * NODES * 8
    row = lax.broadcasted_iota(jnp.int32, (length_of_table, 128), 0) // 8
    wanted = row == rank * NODES + dest_rel
    path = fullest = None
    for n in range(TABLES):
        rows = table_ref[length_of_table * n : length_of_table * (n + 1)]
        every = jnp.dot(rows, from_one, preferred_element_type=f32)
        every = jnp.where(wanted, every, 0.0)
        other = every[0:8]
        for i in range(1, 2 * NODES):
            other = other + every[8 * i : 8 * i + 8]
        uses = jnp.where(link == other[0:1], 1.0, 0.0)
        for hop in range(1, 7):
            uses = uses + jnp.where(link == other[hop : hop + 1], 1.0, 0.0)
        load = jnp.max(jnp.sum(uses, axis=1, keepdims=True), axis=0, keepdims=True)
        if n == 0:
            path, fullest = other, load
        else:
            path = jnp.where(load < fullest, other, path)
            fullest = jnp.minimum(load, fullest)
    me = relative(jnp.zeros((1, 1), jnp.int32) + lax.axis_index("rep"))
    me_z, me_y = me // 2, me % 2
    up, down = (me_z + 1) % RING, (me_z + RING - 1) % RING
    to_me = (down * 2 + me_y, up * 2 + me_y, me_z * 2 + 1 - me_y)
    out_link = [(me * PORTS + k + 1).astype(f32) for k in range(PORTS)]
    in_link = [(to_me[k] * PORTS + k + 1).astype(f32) for k in range(PORTS)]
    tie = (127 - lane).astype(f32)
    hop_row = lax.broadcasted_iota(jnp.int32, (8, 128), 0)
    held = jnp.where(source_rel == me, order, 0).astype(f32)
    home = dest_rel == me
    own_slot = jnp.where(home, source * 2 + rank, 0).astype(f32)
    own_span = jnp.where(home, length, 0.0)
    for ref in (sends, slots, spans):
        ref[...] = jnp.zeros_like(ref)
    fine = []
    for t in range(ROUNDS):
        now = path[0:1]
        if t in TIERS:
            fine.append(jnp.max(now, axis=1, keepdims=True) == 0.0)
        left = jnp.sum(jnp.where(path > 0.0, 1.0, 0.0), axis=0, keepdims=True)
        key = left * 128.0 + tie
        asks = link == now
        first = jnp.max(jnp.where(asks, key, -1.0), axis=1, keepdims=True)
        wins = jnp.where(asks & (first == key), 1.0, 0.0)
        moves = jnp.max(wins, axis=0, keepdims=True) > 0.0
        for k in range(PORTS):
            leaves = moves & (now == out_link[k])
            sends[PORTS * t + k : PORTS * t + k + 1] = jnp.where(leaves, held, 0.0)
        for k in range(PORTS):
            comes = moves & (now == in_link[k])
            held = jnp.where(comes, float(REQS + PORTS * t + k), held)
            slots[PORTS * t + k : PORTS * t + k + 1] = jnp.where(comes, own_slot, 0.0)
            spans[PORTS * t + k : PORTS * t + k + 1] = jnp.where(comes, own_span, 0.0)
        later = jnp.where(hop_row < 7, pltpu.roll(path, 7, axis=0), 0.0)
        path = jnp.where(moves, later, path)
    fine.append(jnp.max(path[0:1], axis=1, keepdims=True) == 0.0)
    tier = sum(jnp.where(done, 0.0, 1.0) for done in fine)
    square = lax.broadcasted_iota(jnp.int32, (128, 128), 0) == lax.broadcasted_iota(
        jnp.int32, (128, 128), 1
    )

    def lay(rows):
        sums = jnp.sum(rows, axis=1, keepdims=True)
        n = rows.shape[0]
        return jnp.sum(jnp.where(square[:n], sums, 0.0), axis=0, keepdims=True)

    slot = lax.broadcasted_iota(jnp.int32, (2 * NODES, 128), 0)
    mine = (slot == source * 2 + rank) & home
    out = [
        lay(sends[...]),
        lay(jnp.where(mine, held, 0.0)),
        lay(jnp.where(mine, length, 0.0)),
        jnp.where(lane >= 0, tier, 0.0),
        lay(slots[...]),
        lay(spans[...]),
        jnp.zeros((2, 128), f32),
    ]
    out_ref[...] = jnp.concatenate(out, axis=0).astype(jnp.int32)


def plan(route, lengths):
    return pl.pallas_call(
        plan_kernel,
        out_shape=jax.ShapeDtypeStruct((8, 128), jnp.int32),
        in_specs=[pl.BlockSpec(memory_space=pltpu.VMEM)] * 2,
        out_specs=pl.BlockSpec(memory_space=pltpu.VMEM),
        scratch_shapes=[pltpu.VMEM((128, 128), jnp.float32)] * 3,
    )(jnp.asarray(path_table(), jnp.bfloat16), jnp.concatenate([route, lengths], axis=0))


def attend(known, new, queries, scale, span):
    f32 = jnp.float32
    bf16 = jnp.bfloat16
    layers = len(known)
    steps, feats = queries[0].shape
    heads = feats // 128
    rows = known[0].shape[0]
    total_rows = rows + new[0].shape[0]
    per_layer = heads * steps
    over = (((1,), (1,)), ((), ()))
    row = lax.broadcasted_iota(jnp.int32, (total_rows, 128), 0)
    lane = lax.broadcasted_iota(jnp.int32, (total_rows, 128), 1)
    even = row % 2 == 0
    part = rows // PARTS
    page = row % part // (part // 2)
    token = PAGE * page + row // part * (PAGE // PARTS) + row % (part // 2) // 2
    fresh = (row >= rows) & ((row - rows) // 2 <= lane % steps)
    valid = even & (((row < rows) & (token < span)) | fresh)
    own_head = lax.broadcasted_iota(jnp.int32, (128, 128), 0)
    own_head = own_head == lax.broadcasted_iota(jnp.int32, (128, 128), 1) // steps
    own_head = jnp.where(own_head, 1.0, 0.0).astype(bf16)
    block = lax.broadcasted_iota(jnp.int32, (per_layer, feats), 1) // 128
    block = block == lax.broadcasted_iota(jnp.int32, (per_layer, feats), 0) // steps

    both = [jnp.concatenate([known[l], new[l]], axis=0) for l in range(layers)]
    query = []
    for one in queries:
        one = jnp.concatenate([one.astype(f32)] * heads, axis=0)
        query.append(jnp.where(block, one, 0.0))
    query.append(jnp.zeros((128 - layers * per_layer, feats), f32))
    query = jnp.concatenate(query, axis=0).astype(bf16)
    score = lax.dot_general(both[0], query, over, preferred_element_type=f32)
    for l in range(1, layers):
        other = lax.dot_general(both[l], query, over, preferred_element_type=f32)
        score = jnp.where(lane // per_layer == l, other, score)
    scale = scale.astype(f32)
    scale = ((scale[0] + scale[1]) + (scale[2] + scale[3])).reshape(4, 128)
    scale = jnp.concatenate([scale, jnp.zeros((12, 128), f32)], axis=0).astype(bf16)
    scale = jnp.dot(scale, own_head, preferred_element_type=f32)
    factor = jnp.where(
        page == 0,
        jnp.where(even, scale[0:1], scale[1:2]),
        jnp.where(even, scale[2:3], scale[3:4]),
    )
    factor = jnp.where(row < rows, factor, 1.0)
    score = jnp.where(valid, score * factor / math.sqrt(128), -jnp.inf)
    power = jnp.exp(score - jnp.max(score, axis=0, keepdims=True))
    total = jnp.sum(power, axis=0, keepdims=True)
    weight = (pltpu.roll(power, 1, axis=0) * factor / total).T
    results = []
    for l in range(layers):
        own = weight[per_layer * l : per_layer * (l + 1)].astype(bf16)
        result = jnp.dot(own, both[l], preferred_element_type=f32)
        parts = [
            result[steps * h : steps * h + steps, 128 * h : 128 * h + 128] for h in range(heads)
        ]
        results.append(jnp.concatenate(parts, axis=1).astype(bf16))
    return results


def exchange_kernel(rounds, plan_ref, table_ref, pages, scales, query_hbm, new_hbm, *refs):
    streams = PARTS + 1
    stores = refs[:streams]
    att = refs[streams]
    refs = refs[streams + 1 :]
    groups = refs[:streams]
    lands = refs[streams : 2 * streams]
    packs = refs[2 * streams : 3 * streams]
    queries, news, group_send, group_recv, send_sem, recv_sem, new_sem = refs[3 * streams :]
    rep = lax.axis_index("rep")
    section = lax.axis_index("section")
    head = lax.axis_index("head")
    tokens = groups[0].shape[2]
    held = pages.shape[2]
    feats = groups[0].shape[4]
    layers, _, steps, _ = queries.shape

    peers = []
    for o in range(16):
        peers.append((lax.rem(section + o // 4, 4), lax.rem(head + o % 4, 4)))
    neighbours = (
        lax.rem(rep + 2, NODES),
        lax.rem(rep + NODES - 2, NODES),
        rep + 1 - 2 * lax.rem(rep, 2),
    )
    barrier = pltpu.get_barrier_semaphore()
    for s, h in peers[1:]:
        pl.semaphore_signal(barrier, inc=1, device_id=(rep, s, h), device_id_type=MESH)
    for n in neighbours:
        pl.semaphore_signal(barrier, inc=1, device_id=(n, section, head), device_id_type=MESH)
    pl.semaphore_wait(barrier, 15 + PORTS)

    def block(i, group):
        if i == PARTS:
            return scales.at[group]
        columns = pl.ds(pl.multiple_of(group * feats, 128), feats)
        return pages.at[0, 0, :, pl.ds(tokens * i, tokens), :, columns]

    def place(i, s, h):
        return groups[i].at[s, pl.ds(held * h, held)]

    def regroup(i, o):
        s, h = peers[o]
        return pltpu.make_async_remote_copy(
            src_ref=block(i, s * 4 + h),
            dst_ref=place(i, section, head),
            send_sem=group_send.at[i, o],
            recv_sem=group_recv.at[i, o],
            device_id=(rep, s, h),
            device_id_type=MESH,
        )

    def regroup_own(i):
        return pltpu.make_async_copy(
            block(i, section * 4 + head), place(i, section, head), group_recv.at[i, 0]
        )

    order = [PARTS] + list(range(PARTS))
    for i in order:
        for o in range(1, 16):
            regroup(i, o).start()
        regroup_own(i).start()
    load_query = pltpu.make_async_copy(query_hbm, queries, new_sem.at[0])
    load_new = pltpu.make_async_copy(new_hbm, news, new_sem.at[1])
    load_query.start()
    load_new.start()

    def send(i, slot, k):
        return pltpu.make_async_remote_copy(
            src_ref=packs[i].at[slot, k],
            dst_ref=lands[i].at[slot, k],
            send_sem=send_sem.at[i, slot, k],
            recv_sem=recv_sem.at[i, slot, k],
            device_id=(neighbours[k], section, head),
            device_id_type=MESH,
        )

    def compose(i, t, slot):
        for k in range(PORTS):
            packs[i][slot, k] = stores[i][plan_ref[0, PORTS * t + k]]
        for k in range(PORTS):
            send(i, slot, k).start()

    def arrive(i, t, slot):
        for k in range(PORTS):
            send(i, slot, k).wait_recv()
        for k in range(PORTS):
            stores[i][REQS + PORTS * t + k] = lands[i][slot, k]

    def attend_unit(at, unit, slot, span):
        known = [
            jnp.concatenate(
                [stores[i][unit, l].reshape(4 * tokens, feats) for i in range(PARTS)], axis=0
            )
            for l in range(layers)
        ]
        new = [news[l, slot].reshape(2 * steps, feats) for l in range(layers)]
        query = [queries[l, slot] for l in range(layers)]
        results = attend(known, new, query, stores[PARTS][unit], span)
        for l in range(layers):
            att[at, l] = results[l]

    def attend_own():
        for c in range(2):
            slot = 2 * rep + c
            attend_unit(c, plan_ref[1, slot], slot, plan_ref[2, slot])

    def attend_arrived(t):
        for k in range(PORTS):
            at = PORTS * t + k
            attend_unit(REQS + at, REQS + at, plan_ref[4, at], plan_ref[5, at])

    lag = OFFSETS + (0,)
    most = max(lag)

    def first(i):
        regroup_own(i).wait()
        for o in range(1, 16):
            regroup(i, o).wait_recv()
        for q in range(REQS):
            for j in range(2):
                stores[i][q, :, j] = groups[i][:, table_ref[0, 2 * q + j]]
        compose(i, 0, 0)

    def attend_at(time, k):
        if isinstance(time, int) and not 0 < time - most <= rounds:
            return
        at = PORTS * (time - most - 1) + k
        attend_unit(REQS + at, REQS + at, plan_ref[4, at], plan_ref[5, at])

    def beat(time):
        for n, i in enumerate(order):
            t = time - lag[i]
            if not isinstance(time, int):
                slot = lax.rem(t, 2)
                arrive(i, t - 1, 1 - slot)
                for k in range(PORTS):
                    send(i, slot, k).wait_send()
                compose(i, t, slot)
            elif t == 0:
                first(i)
            elif 0 < t <= rounds:
                arrive(i, t - 1, (t - 1) % 2)
                if t >= 2 and t < rounds:
                    for k in range(PORTS):
                        send(i, t % 2, k).wait_send()
                if t < rounds:
                    compose(i, t, t % 2)
            if n == PARTS:
                for k in range(PORTS):
                    attend_at(time, k)

    for time in range(most + 2):
        beat(time)
        if time == most:
            load_query.wait()
            load_new.wait()
            attend_own()

    def one(time, carry):
        beat(time)
        return carry

    lax.fori_loop(most + 2, rounds, one, 0)
    for time in range(rounds, rounds + most + 2):
        beat(time)
    for i in order:
        for slot in range(2):
            for k in range(PORTS):
                send(i, slot, k).wait_send()
        for o in range(1, 16):
            regroup(i, o).wait_send()


def exchange(rounds, steps, page_table, pages, scales, queries, new_kv):
    layers, nodes, cap, step_count, feats = queries.shape[1:]
    held = pages.shape[2]
    tokens = pages.shape[3] // PARTS
    store = REQS + PORTS * rounds
    units = [(tokens, 2, feats)] * PARTS + [(2, 128)]
    bf16 = jnp.bfloat16
    anywhere = pl.BlockSpec(memory_space=pl.ANY)
    smem = pl.BlockSpec(memory_space=pltpu.SMEM)
    vmem = pl.BlockSpec(memory_space=pltpu.VMEM)
    scratch = [pltpu.VMEM((layers, 4 * held) + u, bf16) for u in units]
    scratch += [pltpu.VMEM((2, PORTS, layers, 2) + u, bf16) for u in units] * 2
    query_shape = (layers, nodes * cap, step_count, feats)
    new_shape = (layers, nodes * cap, step_count, 2, feats)
    scratch += [pltpu.VMEM(query_shape, bf16), pltpu.VMEM(new_shape, bf16)]
    dma = pltpu.SemaphoreType.DMA
    streams = PARTS + 1
    scratch += [dma((streams, 16)), dma((streams, 16))]
    scratch += [dma((streams, 2, PORTS)), dma((streams, 2, PORTS)), dma((2,))]
    return pl.pallas_call(
        functools.partial(exchange_kernel, rounds),
        out_shape=[jax.ShapeDtypeStruct((store, layers, 2) + u, bf16) for u in units]
        + [jax.ShapeDtypeStruct((store, layers, step_count, feats), bf16)],
        in_specs=[smem, smem] + [anywhere] * 4,
        out_specs=[vmem] * (streams + 1),
        scratch_shapes=scratch,
        compiler_params=pltpu.CompilerParams(
            collective_id=rounds, has_side_effects=True, vmem_limit_bytes=40 << 20
        ),
        cost_estimate=pl.CostEstimate(flops=0, bytes_accessed=20 << 20, transcendentals=0),
    )(
        steps,
        page_table,
        pages,
        scales,
        queries.reshape(query_shape),
        new_kv.reshape(new_shape),
    )


def place_kernel(plan_ref, *refs):
    units, scales, att = refs[:PARTS], refs[PARTS], refs[PARTS + 1]
    cache_hbm, scales_ref, att_hbm, zero_unit, zero_att, sems = refs[PARTS + 2 :]
    layers, slots, _, _, heads = scales_ref.shape
    tokens = units[0].shape[3]
    cap = 2
    rep = lax.axis_index("rep")
    zero_unit[...] = jnp.zeros_like(zero_unit)
    zero_att[...] = jnp.zeros_like(zero_att)

    def copies(i, live):
        unit = plan_ref[1, i]
        at = jnp.where(i // cap == rep, i % cap, unit)
        out = []
        for s in range(PARTS):
            to = cache_hbm.at[0, :, i // cap, i % cap, :, pl.ds(tokens * s, tokens)]
            source = units[s].at[unit] if live else zero_unit
            out.append(pltpu.make_async_copy(source, to, sems.at[i, s]))
        source = att.at[at] if live else zero_att
        to = att_hbm.at[0, :, i // cap, i % cap]
        return out + [pltpu.make_async_copy(source, to, sems.at[i, PARTS])]

    @pl.loop(0, slots)
    def _(i):
        @pl.when(plan_ref[2, i] > 0)
        def _():
            for copy in copies(i, True):
                copy.start()
            scale = scales[plan_ref[1, i]]
            for l in range(layers):
                scales_ref[l, i] = scale[l][:, :, heads * l : heads * l + heads]

        @pl.when(plan_ref[2, i] == 0)
        def _():
            for copy in copies(i, False):
                copy.start()
            for l in range(layers):
                scales_ref[l, i] = jnp.zeros((2, 2, heads), scales_ref.dtype)

    @pl.loop(0, slots)
    def _(i):
        for copy in copies(i, False):
            copy.wait()


def place(steps, units, queries):
    layers, nodes, cap, step_count, feats = queries.shape[1:]
    heads = feats // 128
    bf16 = jnp.bfloat16
    anywhere = pl.BlockSpec(memory_space=pl.ANY)
    vmem = pl.BlockSpec(memory_space=pltpu.VMEM)
    smem = pl.BlockSpec(memory_space=pltpu.SMEM)
    cache, scales, attention = pl.pallas_call(
        place_kernel,
        in_specs=[smem] + [vmem] * len(units),
        out_specs=[anywhere, vmem, anywhere],
        out_shape=[
            jax.ShapeDtypeStruct((1, layers, nodes, cap, 2, PAGE, 2, feats), bf16),
            jax.ShapeDtypeStruct((layers, nodes * cap, 2, 2, heads), bf16),
            jax.ShapeDtypeStruct(queries.shape, bf16),
        ],
        scratch_shapes=[
            pltpu.VMEM(units[0].shape[1:], bf16),
            pltpu.VMEM(units[PARTS + 1].shape[1:], bf16),
            pltpu.SemaphoreType.DMA((nodes * cap, PARTS + 1)),
        ],
        compiler_params=pltpu.CompilerParams(vmem_limit_bytes=40 << 20),
    )(steps, *units)
    cache = cache.reshape(1, layers, nodes, cap, 2 * PAGE, 2, feats)
    return cache, scales.reshape(1, layers, nodes, cap, 2, 2, heads), attention


def slot_ranks(route):
    req_ids = jnp.arange(route.shape[1], dtype=jnp.int32)
    same_dest = route[:, :, None] == route[:, None, :]
    earlier = req_ids[None, :] < req_ids[:, None]
    return jnp.sum((same_dest & earlier[None]).astype(jnp.int32), axis=2)


def padded(prompt_pages, page_scales, page_table, lengths, route, queries, new_kv):
    rep_count = lax.axis_size("rep")
    section_count = lax.axis_size("section")
    head_count = lax.axis_size("head")
    replica = lax.axis_index("rep")
    layers_here = prompt_pages.shape[1]
    pages_here = prompt_pages.shape[2]
    page_rows = prompt_pages.shape[3]
    feature_count = prompt_pages.shape[5]
    heads_total = page_scales.shape[4]
    head_dim = feature_count // heads_total
    group_count = section_count * head_count
    feat_here = feature_count // group_count
    heads_here = heads_total // group_count
    req_count = route.shape[1]
    capacity = max(2, req_count // rep_count)
    pages_each = page_table.shape[1] // req_count
    layer_count = layers_here * section_count
    span_max = page_rows * pages_each
    steps_count = queries.shape[4]
    req_ids = jnp.arange(req_count, dtype=jnp.int32)
    dest_ids = jnp.arange(rep_count, dtype=jnp.int32)
    cap_ids = jnp.arange(capacity, dtype=jnp.int32)
    page_ids = jnp.arange(pages_each, dtype=jnp.int32)
    slot_rank = slot_ranks(route)
    own_route = lax.dynamic_index_in_dim(route, replica, 0, keepdims=False)
    own_rank = lax.dynamic_index_in_dim(slot_rank, replica, 0, keepdims=False)
    send_match = (own_route[None, None, :] == dest_ids[:, None, None]) & (
        own_rank[None, None, :] == cap_ids[None, :, None]
    )
    send_live = jnp.any(send_match, axis=2)
    send_request = jnp.sum(jnp.where(send_match, req_ids[None, None, :], 0), axis=2)
    physical = page_table[0][send_request[:, :, None] * pages_each + page_ids[None, None, :]]
    recv_match = (route[:, None, :] == replica) & (slot_rank[:, None, :] == cap_ids[None, :, None])
    recv_live = jnp.any(recv_match, axis=2)
    slot_span = jnp.sum(jnp.where(recv_match, lengths[:, None, :], 0), axis=2)
    page_view = prompt_pages[0].reshape(
        layers_here, pages_here, page_rows, 2, section_count, head_count, feat_here
    )
    scale_view = page_scales[0].reshape(
        layers_here, pages_here, 1, 2, section_count, head_count, heads_here
    )
    zero_page = jnp.zeros((), prompt_pages.dtype)
    zero_scale = jnp.zeros((), page_scales.dtype)
    regrouped = (
        lax.all_to_all(
            lax.all_to_all(page_view, "section", split_axis=4, concat_axis=0, tiled=True),
            "head",
            split_axis=5,
            concat_axis=1,
            tiled=True,
        ),
        lax.all_to_all(
            lax.all_to_all(scale_view, "section", split_axis=4, concat_axis=0, tiled=True),
            "head",
            split_axis=5,
            concat_axis=1,
            tiled=True,
        ),
    )
    all_pages = regrouped[0].reshape(layer_count, pages_here * head_count, page_rows, 2, feat_here)
    all_scales = regrouped[1].reshape(layer_count, pages_here * head_count, 1, 2, heads_here)
    live_mask = send_live[None, :, :, None, None, None, None]
    slot_pages = jnp.where(live_mask, all_pages[:, physical], zero_page)
    slot_scales = jnp.where(live_mask, all_scales[:, physical], zero_scale)
    received = (
        lax.all_to_all(slot_pages, "rep", split_axis=1, concat_axis=1, tiled=True),
        lax.all_to_all(slot_scales, "rep", split_axis=1, concat_axis=1, tiled=True),
    )
    page_cache = received[0].reshape(layer_count, rep_count, capacity, span_max, 2, feat_here)
    scale_cache = received[1].reshape(layer_count, rep_count, capacity, pages_each, 2, heads_here)
    prompt_keys = page_cache[:, :, :, :, 0, :].reshape(
        layer_count, rep_count, capacity, span_max, heads_here, head_dim
    )
    prompt_values = page_cache[:, :, :, :, 1, :].reshape(
        layer_count, rep_count, capacity, span_max, heads_here, head_dim
    )
    query_rows = queries[0].reshape(
        layer_count, rep_count, capacity, steps_count, heads_here, head_dim
    )
    new_keys = new_kv[0][:, :, :, :, 0, :].reshape(
        layer_count, rep_count, capacity, steps_count, heads_here, head_dim
    )
    new_values = new_kv[0][:, :, :, :, 1, :].reshape(
        layer_count, rep_count, capacity, steps_count, heads_here, head_dim
    )
    score_root = math.sqrt(head_dim)
    key_scale = jnp.transpose(scale_cache[:, :, :, :, 0, :], (0, 1, 2, 4, 3))
    value_scale = jnp.transpose(scale_cache[:, :, :, :, 1, :], (0, 1, 2, 4, 3))
    prompt_dots = jnp.einsum(
        "lrcthd,lrckhd->lrchtk", query_rows, prompt_keys, preferred_element_type=jnp.float32
    )
    prompt_dots = prompt_dots.reshape(
        layer_count, rep_count, capacity, heads_here, steps_count, pages_each, page_rows
    )
    prompt_score = (
        prompt_dots * key_scale[:, :, :, :, None, :, None].astype(jnp.float32) / score_root
    )
    prompt_score = prompt_score.reshape(
        layer_count, rep_count, capacity, heads_here, steps_count, span_max
    )
    fresh_score = (
        jnp.einsum(
            "lrcthd,lrcuhd->lrchtu", query_rows, new_keys, preferred_element_type=jnp.float32
        )
        / score_root
    )
    visible = (jnp.arange(span_max, dtype=jnp.int32)[None, None, :] < slot_span[:, :, None])[
        None, :, :, None, None, :
    ]
    causal = (
        jnp.arange(steps_count, dtype=jnp.int32)[None, :]
        <= jnp.arange(steps_count, dtype=jnp.int32)[:, None]
    )
    row_max = jnp.maximum(
        jnp.max(jnp.where(visible, prompt_score, -jnp.inf), axis=-1, keepdims=True),
        jnp.max(jnp.where(causal, fresh_score, -jnp.inf), axis=-1, keepdims=True),
    )
    exp_prompt = jnp.where(visible, jnp.exp(prompt_score - row_max), 0.0)
    exp_fresh = jnp.where(causal, jnp.exp(fresh_score - row_max), 0.0)
    row_total = jnp.sum(exp_prompt, axis=-1, keepdims=True) + jnp.sum(
        exp_fresh, axis=-1, keepdims=True
    )
    value_weight = jnp.broadcast_to(
        value_scale[:, :, :, :, :, None], value_scale.shape + (page_rows,)
    )
    value_weight = value_weight.reshape(layer_count, rep_count, capacity, heads_here, span_max)[
        :, :, :, :, None, :
    ]
    prompt_weight = (exp_prompt * value_weight.astype(jnp.float32) / row_total).astype(jnp.bfloat16)
    fresh_weight = (exp_fresh / row_total).astype(jnp.bfloat16)
    attended = jnp.einsum(
        "lrchtk,lrckhd->lrcthd", prompt_weight, prompt_values, preferred_element_type=jnp.float32
    )
    attended = attended + jnp.einsum(
        "lrchtu,lrcuhd->lrcthd", fresh_weight, new_values, preferred_element_type=jnp.float32
    )
    attended = jnp.where(recv_live[None, :, :, None, None, None], attended, 0.0).astype(
        jnp.bfloat16
    )
    return (
        page_cache.reshape(1, layer_count, rep_count, capacity, span_max, 2, feat_here),
        scale_cache.reshape(1, layer_count, rep_count, capacity, pages_each, 2, heads_here),
        attended.reshape(1, layer_count, rep_count, capacity, steps_count, feat_here),
    )


def body(prompt_pages, page_scales, page_table, lengths, route, queries, new_kv):
    steps = plan(route, lengths)

    def direct(rounds, prompt_pages, page_scales, page_table, lengths, route, queries, new_kv):
        held = page_scales.shape[2]
        scales = page_scales.reshape(held, 2, 16, -1).transpose(2, 0, 1, 3)
        heads = scales.shape[3]
        scales = jnp.pad(jnp.tile(scales, (1, 1, 1, 4)), ((0, 0),) * 3 + ((0, 128 - 4 * heads),))
        own = jnp.arange(128) // heads == lax.axis_index("section")
        scales = jnp.where(own, scales, jnp.zeros((), scales.dtype))
        units = exchange(rounds, steps, page_table, prompt_pages, scales, queries, new_kv)
        return tuple(place(steps, units, queries))

    return lax.switch(
        len(TIERS) - steps[3, 0],
        [padded] + [functools.partial(direct, rounds) for rounds in TIERS[::-1]],
        prompt_pages,
        page_scales,
        page_table,
        lengths,
        route,
        queries,
        new_kv,
    )


def solution(mesh):
    return jax.shard_map(
        body,
        mesh=mesh,
        in_specs=(
            P("rep", "section", "head", None, None, None),
            P("rep", "section", "head", None, None),
            P("rep", None),
            P(),
            P(),
            P("rep", None, None, None, None, ("section", "head")),
            P("rep", None, None, None, None, None, ("section", "head")),
        ),
        out_specs=(
            P("rep", None, None, None, None, None, ("section", "head")),
            P("rep", None, None, None, None, None, ("section", "head")),
            P("rep", None, None, None, None, ("section", "head")),
        ),
        check_vma=False,
    )
```
